32 devices in a mesh: dp: 8 (over z, y), kv: 4 (over x, core).
Axes of the slice: x: 2, y: 2, z: 4, core: 2. Of those that a mesh axis runs over, the one named last changes fastest.
Arguments:
- residual_in: bfloat16 [2048, 1536], P(('dp', 'kv')), may hold values from -30 to 30
- queries: bfloat16 [2048, 1536], P('dp'), may hold values from -13 to 13
- key_cache: bfloat16 [24, 4096, 512], P('dp', 'kv'), may hold values from -16 to 16
- value_cache: bfloat16 [24, 4096, 512], P('dp', 'kv'), may hold values from -4 to 4
- cache_lengths: int32 [24], P('dp'), may hold values from 2 to 4096, as said below
- out_weight: bfloat16 [1536, 1536], P('kv'), may hold values from -0.15625 to 0.15625
- norm_gain: float32 [1536], replicated, may hold values from 0.1 to 1.9
- gate_weight: bfloat16 [1536, 6912], P('dp', 'kv'), may hold values from -0.15625 to 0.15625
- up_weight: bfloat16 [1536, 6912], P('dp', 'kv'), may hold values from -0.15625 to 0.15625
- down_weight: bfloat16 [6912, 1536], P('kv', 'dp'), may hold values from -0.078125 to 0.078125
Outputs:
- layer_out: bfloat16 [2048, 1536], P(('dp', 'kv'))
The draws below stay inside these ranges and needn't reach their ends.
Inputs may be any that keep to these rules, and one draw needn't show every extreme that they name: `cache_lengths`: for the first request of each block of 3 (the prefill span) the length lies between 255 and 4096; for the others between 2 and 4096. In every block of 3 requests some decode request has length exactly 4096.
All inputs are finite; a program needn't handle non-finite values.
Results may differ from the reference program's by a relative error of at most 0.013.
Values may be sent and summed in bfloat16 or wider, within the bound.
No kernel may reach another device: no remote copies, remote signals or barrier semaphores. Data moves between devices by JAX's collectives and lax.ppermute only.
A program may use at most 128 MiB of HBM per device.

```python
import jax
import jax.numpy as jnp
from jax import lax

D = 1536
H = 24
HD = 64
KVH = 8
FF = 6912
CTX = 4096
ROWS_DP = 256
SPAN = 254
REQS = 3
REQUESTS = 24
TOKENS = 2048
SLAB = 1024
N_DP = 8
N_KV = 4


def draw_queries(key, part):
    noise_key = jax.random.fold_in(key, 11)
    values = jnp.clip(jax.random.normal(noise_key, (TOKENS, H * HD), jnp.float32), -4.0, 4.0)
    return values.astype(jnp.bfloat16)


def draw_key_cache(key, part):
    noise_key = jax.random.fold_in(key, 23)
    values = jnp.clip(jax.random.normal(noise_key, (REQUESTS, CTX, KVH * HD), jnp.float32), -4.0, 4.0)
    return values.astype(jnp.bfloat16)


def draw_cache_lengths(key, part):
    first_key, second_key, third_key, fourth_key = jax.random.split(jax.random.fold_in(key, 31), 4)
    factor_one = jax.random.randint(first_key, (REQUESTS,), 1, CTX + 1)
    factor_two = jax.random.randint(second_key, (REQUESTS,), 1, CTX + 1)
    decode_length = jnp.maximum(factor_one * factor_two // CTX, 2)
    offsets = jax.random.randint(third_key, (REQUESTS,), 1, CTX - SPAN + 1)
    longest = jax.random.randint(fourth_key, (REQUESTS // REQS,), 1, REQS)
    request = jnp.arange(REQUESTS, dtype=jnp.int32)
    within = request % REQS
    owner = request // REQS
    lengths = jnp.where(within == 0, offsets + SPAN, jnp.where(within == longest[owner], CTX, decode_length))
    return lengths.astype(jnp.int32)


def draw_residual_in(key, part):
    first_key, second_key, third_key = jax.random.split(jax.random.fold_in(key, 41), 3)
    row_scale = jnp.exp(jax.random.uniform(first_key, (TOKENS, 1), jnp.float32, -1.15, 1.15))
    column_scale = jnp.exp(jax.random.uniform(second_key, (1, D), jnp.float32, -1.15, 1.15))
    values = jnp.clip(jax.random.normal(third_key, (TOKENS, D), jnp.float32), -3.0, 3.0)
    return (values * row_scale * column_scale).astype(jnp.bfloat16)


def steps_of(key, extent, shards, low, largest):
    def one(position, blocks):
        draws = jax.random.uniform(jax.random.fold_in(jax.random.fold_in(key, 6), position), (blocks,), jnp.float32, low / len(shards), largest / len(shards))
        return jnp.repeat(jnp.exp(draws), extent[position] // blocks).reshape((-1,) + (1,) * (len(extent) - position - 1))

    gain = one(*shards[0])
    for cut in shards[1:]:
        gain = gain * one(*cut)
    return gain


def normal_values(own_key, extent, scale, reach, cuts=(), kind=jnp.bfloat16):
    array = scale * jax.random.normal(own_key, extent, jnp.float32)
    if cuts:
        array = array * steps_of(own_key, extent, cuts, -0.22, 0.18)
    return jnp.clip(array, -reach, reach).astype(kind)


def setup_inputs(seed: int = 0) -> dict:
    splits = jax.random.split(jax.random.key(seed), 11)
    return {
        "residual_in": draw_residual_in(jax.random.fold_in(splits[10], 71), 0),
        "queries": draw_queries(jax.random.fold_in(splits[10], 71), 0),
        "key_cache": draw_key_cache(jax.random.fold_in(splits[10], 71), 0),
        "value_cache": normal_values(splits[3], (REQUESTS, CTX, KVH * HD), 1.0, 4.0, ((0, 8), (1, 4))),
        "cache_lengths": draw_cache_lengths(jax.random.fold_in(splits[10], 71), 0),
        "out_weight": normal_values(splits[5], (H * HD, D), (H * HD) ** -0.5, 0.15625, ((0, 4),)),
        "norm_gain": jnp.clip(1.0 + 0.18 * jax.random.normal(splits[6], (D,), jnp.float32), 0.1, 1.9),
        "gate_weight": normal_values(splits[7], (D, FF), D ** -0.5, 0.15625, ((0, 8), (1, 4))),
        "up_weight": normal_values(splits[8], (D, FF), D ** -0.5, 0.15625, ((0, 8), (1, 4))),
        "down_weight": normal_values(splits[9], (FF, D), FF ** -0.5, 0.078125, ((0, 4), (1, 8))),
    }


def partials(query_rows, keys, values, lengths, first_key):
    row_count = query_rows.shape[0]
    request_count = keys.shape[0]
    slab_width = keys.shape[1]
    group_size = H // KVH
    span_rows = row_count - (request_count - 1)
    query_heads = query_rows.reshape(row_count, KVH, group_size, HD)
    key_heads = keys.reshape(request_count, slab_width, KVH, HD)
    value_heads = values.reshape(request_count, slab_width, KVH, HD)
    score_scale = HD ** (-0.5)
    key_place = first_key + jnp.arange(slab_width, dtype=jnp.int32)
    score_first = jnp.einsum('tgcd,pgd->tgcp', query_heads[:span_rows], key_heads[0], preferred_element_type=jnp.float32)
    score_rest = jnp.einsum('rgcd,rpgd->rgcp', query_heads[span_rows:], key_heads[1:], preferred_element_type=jnp.float32)
    scores = jnp.concatenate([score_first, score_rest], 0) * score_scale
    limits = jnp.concatenate([lengths[0] - span_rows + jnp.arange(span_rows, dtype=jnp.int32), lengths[1:] - 1])
    usable = (key_place[None, :] <= limits[:, None])[:, None, None, :]
    top_score = lax.optimization_barrier(jnp.max(jnp.where(usable, scores, -1e+30), axis=-1))
    weights = jnp.where(usable, jnp.exp(scores - top_score[..., None]), 0.0)
    weight_sum = lax.optimization_barrier(jnp.sum(weights, axis=-1))
    weight_low = weights.astype(jnp.bfloat16)
    acc_first = jnp.einsum('tgcp,pgd->tgcd', weight_low[:span_rows], value_heads[0], preferred_element_type=jnp.float32)
    acc_rest = jnp.einsum('rgcp,rpgd->rgcd', weight_low[span_rows:], value_heads[1:], preferred_element_type=jnp.float32)
    weighted = jnp.concatenate([acc_first, acc_rest], 0).reshape(row_count, H * HD)
    return (top_score.reshape(row_count, H), weight_sum.reshape(row_count, H), weighted)

def combine(earlier, later):
    joined_top = jnp.maximum(earlier[0], later[0])
    scale_first = jnp.exp(earlier[0] - joined_top)
    scale_second = jnp.exp(later[0] - joined_top)
    weight_sum = earlier[1] * scale_first + later[1] * scale_second
    weighted = earlier[2] * jnp.repeat(scale_first, HD, axis=-1) + later[2] * jnp.repeat(scale_second, HD, axis=-1)
    return (joined_top, weight_sum, weighted)

def reference(residual_in, queries, key_cache, value_cache, cache_lengths, out_weight, norm_gain, gate_weight, up_weight, down_weight):
    query_blocks = queries.reshape(N_DP, ROWS_DP, H * HD)
    key_blocks = key_cache.reshape(N_DP, REQS, N_KV, SLAB, KVH * HD)
    value_blocks = value_cache.reshape(N_DP, REQS, N_KV, SLAB, KVH * HD)
    length_blocks = cache_lengths.reshape(N_DP, REQS)
    residual_blocks = residual_in.reshape(N_DP, ROWS_DP, D)

    def layer_block(operands):
        query_rows, keys, values, lengths, residual_rows = operands
        state = partials(query_rows, keys[:, 0], values[:, 0], lengths, 0)
        for slab_index in range(1, N_KV):
            state = combine(state, partials(query_rows, keys[:, slab_index], values[:, slab_index], lengths, slab_index * SLAB))
        attended = (state[2] / jnp.repeat(state[1], HD, axis=-1)).astype(jnp.bfloat16)
        mixed = jnp.dot(attended, out_weight, preferred_element_type=jnp.float32)
        residual = (residual_rows.astype(jnp.float32) + mixed).astype(jnp.bfloat16)
        wide = residual.astype(jnp.float32)
        normed = (wide * lax.rsqrt(lax.optimization_barrier(jnp.mean(wide * wide, axis=-1, keepdims=True)) + 1e-05) * norm_gain).astype(jnp.bfloat16)
        gate_sum = jnp.dot(normed, gate_weight, preferred_element_type=jnp.float32)
        up_sum = jnp.dot(normed, up_weight, preferred_element_type=jnp.float32)
        hidden = (jax.nn.silu(gate_sum) * up_sum).astype(jnp.bfloat16)
        mlp = jnp.dot(hidden, down_weight, preferred_element_type=jnp.float32)
        return (wide + mlp).astype(jnp.bfloat16)
    layer_out = lax.map(layer_block, (query_blocks, key_blocks, value_blocks, length_blocks, residual_blocks))
    return layer_out.reshape(TOKENS, D)
```

```python
import functools

import jax
import jax.numpy as jnp
from jax import lax
from jax.experimental import pallas as pl
from jax.experimental.pallas import tpu as pltpu
from jax.sharding import PartitionSpec as P

H = 24
HD = 64
KVH = 8
LANES = 128
SUM_HIGH = 32
SUM_LOW = 64
OUTER = 4

VMEM = pl.BlockSpec(memory_space=pltpu.VMEM)
SMEM = pl.BlockSpec(memory_space=pltpu.SMEM)
NT = (((1,), (1,)), ((), ()))
BF16 = jnp.bfloat16
F32 = jnp.float32


def params(mib=48):
    return pltpu.CompilerParams(vmem_limit_bytes=mib * 1024 * 1024)


def iota(shape, dim):
    return lax.broadcasted_iota(jnp.int32, shape, dim)


def dot(a, b):
    return jnp.dot(a, b, preferred_element_type=F32)


def one_hot(condition):
    return jnp.where(condition, 1.0, 0.0).astype(BF16)


def pack_kernel(main, tail, z_ref, gate_ref, up_ref, down_ref, *outs):
    rows = gate_ref.shape[0]
    width = down_ref.shape[1]
    tail_at = OUTER * main
    gate_tail = gate_ref[:, tail_at:]
    up_tail = up_ref[:, tail_at:]
    for shift in range(OUTER):
        target = lax.rem(z_ref[0] + shift, OUTER)
        out, down_out = outs[shift], outs[OUTER + shift]
        column = pl.multiple_of(target * main, LANES)
        out[:, :main] = gate_ref[:, pl.ds(column, main)]
        out[:, main : 2 * main] = up_ref[:, pl.ds(column, main)]
        shape = (OUTER * tail, LANES)
        k, lane = iota(shape, 0), iota(shape, 1)
        pick_gate = one_hot((lane < tail) & (k == lane + target * tail))
        pick_up = one_hot((lane >= tail) & (lane < 2 * tail) & (k == lane - tail + target * tail))
        out[:, 2 * main :] = (dot(gate_tail, pick_gate) + dot(up_tail, pick_up)).astype(BF16)
        down_main = down_ref[pl.ds(pl.multiple_of(target * main, 16), main), :]
        down_tail = down_ref[pl.ds(pl.multiple_of(tail_at + target * tail, 16), tail), :]
        shape = (width, 2 * width)
        k, lane = iota(shape, 0), iota(shape, 1)
        low, high = one_hot(k == lane), one_hot(k == lane - width)
        half = main // 2
        down_out[:half, :] = (dot(down_main[:half], low) + dot(down_main[half:], high)).astype(BF16)
        down_out[half:, :] = dot(down_tail, low).astype(BF16)


def unpack_kernel(main, tail, at_ref, *refs):
    parts = 2 * OUTER
    gate_up, down, out, down_out = refs[:parts], refs[parts : 2 * parts], refs[-2], refs[-1]
    rows = gate_up[0].shape[0]
    width = down[0].shape[1] // 2
    half = main // 2
    out_rows = down_out.shape[0]
    shape = (2 * width, 2 * width)
    k, lane = iota(shape, 0), iota(shape, 1)
    high = at_ref[1]
    for shift in range(OUTER):
        source = lax.rem(at_ref[0] + OUTER - shift, OUTER)
        column = pl.multiple_of(source * 2 * width, LANES)
        top = bottom = end = None
        for part in range(2):
            index = 2 * shift + part
            place = high if part == 0 else 1 - high
            row = pl.multiple_of((source * 2 + place) * rows, 16)
            out[pl.ds(row, rows), :] = gate_up[index][...]
            move = place * width
            inside = (lane >= move) & (lane < move + width)
            pick_top = one_hot(inside & (k == lane - move))
            pick_bottom = one_hot(inside & (k == lane - move + width))
            block = down[index][...]
            a, b, c = dot(block[:half], pick_top), dot(block[:half], pick_bottom), dot(block[half:], pick_top)
            top, bottom, end = (a, b, c) if top is None else (top + a, bottom + b, end + c)
        down_out[:half, pl.ds(column, 2 * width)] = top.astype(BF16)
        down_out[half:main, pl.ds(column, 2 * width)] = bottom.astype(BF16)
        down_out[main : main + tail, pl.ds(column, 2 * width)] = end.astype(BF16)
    down_out[main + tail :, :] = jnp.zeros((out_rows - main - tail, down_out.shape[1]), BF16)


def attention_kernel(at_ref, q_ref, k_ref, v_ref, keep_ref, send_ref, bias, result, stats):
    step = pl.program_id(0)
    rows, block = q_ref.shape
    requests, slab, _ = k_ref.shape
    span = rows - (requests - 1)
    heads = block // HD
    group = H // KVH
    first_key, half_row = at_ref[0], at_ref[1]

    @pl.when(step == 0)
    def _():
        place = first_key + iota((rows, slab), 1)
        limit = at_ref[2] - span + iota((rows, slab), 0)
        bias[...] = jnp.where(place <= limit, 0.0, -1e30)
        stats[...] = jnp.zeros_like(stats)

    lane = iota((1, LANES), 1)
    low_lanes = lane < HD

    def in_half(a):
        return low_lanes if a == 0 else ~low_lanes

    def aligned(h):
        tile = q_ref[:, (h // 2) * LANES : (h // 2 + 1) * LANES].astype(F32) * HD**-0.5
        a = h // group
        if h % 2 != a:
            tile = pltpu.roll(tile, HD, 1)
        return jnp.where(in_half(a), tile, 0.0)

    def placed(value, h):
        return pltpu.roll(value, HD, 1) if h % 2 != h // group else value

    def record(old, h, top, total):
        column = step * heads + h
        high = total.astype(BF16).astype(F32)
        old = jnp.where(lane == column, top, old)
        old = jnp.where(lane == column + SUM_HIGH, high, old)
        return jnp.where(lane == column + SUM_LOW, total - high, old)

    keys = k_ref[0]
    values = [jnp.where(in_half(a), v_ref[0], jnp.ones((), BF16)) for a in range(2)]
    stat = stats[...]
    decode = []
    outs = []
    for h in range(heads):
        a = h // group
        query = aligned(h)
        decode.append(query[rows - 8 :])
        scores = lax.dot_general(query.astype(BF16), keys, NT, preferred_element_type=F32) + bias[...]
        top = jnp.maximum(jnp.max(scores, axis=1, keepdims=True), -1e29).astype(BF16).astype(F32)
        weights = jnp.exp(scores - top).astype(BF16)
        out = dot(weights, values[a])
        total = jnp.where(in_half(a), pltpu.roll(out, HD, 1), out)
        stat = record(stat, h, top, total)
        outs.append(placed(out, h))
        if h % 2 == 1:
            result[:, (h // 2) * LANES : (h // 2 + 1) * LANES] = jnp.where(low_lanes, outs[h - 1], outs[h])
    stats[...] = stat

    sub = iota((16, 1), 0)
    for r in range(1, requests):
        row = rows - requests + r
        query = jnp.zeros((16, LANES), F32)
        for h in range(heads):
            line = decode[h][8 - requests + r : 9 - requests + r]
            query = jnp.where(sub == h, jnp.broadcast_to(line, (16, LANES)), query)
        scores = lax.dot_general(query.astype(BF16), k_ref[r], NT, preferred_element_type=F32)
        usable = first_key + iota((16, slab), 1) < at_ref[2 + r]
        scores = jnp.where(usable, scores, -1e30)
        top = jnp.maximum(jnp.max(scores, axis=1, keepdims=True), -1e29).astype(BF16).astype(F32)
        weights = jnp.exp(scores - top)
        total = jnp.sum(weights, axis=1, keepdims=True)
        out = dot(weights.astype(BF16), v_ref[r])
        line = stats[row : row + 1, :]
        for h in range(heads):
            line = record(line, h, top[h : h + 1], total[h : h + 1])
        stats[row : row + 1, :] = line
        for h in range(1, heads, 2):
            pair = jnp.where(low_lanes, placed(out[h - 1 : h], h - 1), placed(out[h : h + 1], h))
            result[row : row + 1, (h // 2) * LANES : (h // 2 + 1) * LANES] = pair

    quarter = rows // 4
    column = pl.multiple_of(step * block, LANES)
    for ref, which in ((keep_ref, half_row), (send_ref, 1 - half_row)):
        for part in range(2):
            row = pl.multiple_of((2 * part + which) * quarter, 16)
            ref[part * quarter : (part + 1) * quarter, pl.ds(column, block)] = result[
                pl.ds(row, quarter), :
            ].astype(BF16)

    @pl.when(step == pl.num_programs(0) - 1)
    def _():
        for ref, which in ((keep_ref, half_row), (send_ref, 1 - half_row)):
            for part in range(2):
                row = pl.multiple_of((2 * part + which) * quarter, 16)
                ref[part * quarter : (part + 1) * quarter, H * HD :] = stats[pl.ds(row, quarter), :].astype(BF16)


def attention(queries, keys, values, at):
    rows, width = queries.shape
    requests, slab, _ = keys.shape
    block = 2 * (H // KVH) * HD
    half = jax.ShapeDtypeStruct((rows // 2, width + LANES), BF16)
    whole = pl.BlockSpec((rows // 2, width + LANES), lambda g: (0, 0))
    return pl.pallas_call(
        attention_kernel,
        grid=(width // block,),
        in_specs=[
            SMEM,
            pl.BlockSpec((rows, block), lambda g: (0, g)),
            pl.BlockSpec((requests, slab, LANES), lambda g: (0, 0, g)),
            pl.BlockSpec((requests, slab, LANES), lambda g: (0, 0, g)),
        ],
        out_specs=[whole, whole],
        out_shape=[half, half],
        scratch_shapes=[
            pltpu.VMEM((rows, slab), F32),
            pltpu.VMEM((rows, block), F32),
            pltpu.VMEM((rows, LANES), F32),
        ],
        compiler_params=params(),
        cost_estimate=pl.CostEstimate(
            flops=4 * rows * width * slab * 4, bytes_accessed=8 * 1024 * 1024, transcendentals=rows * H * slab
        ),
        name="attention",
    )(at, queries, keys, values)


def expanded(scale, width):
    high = scale.astype(BF16).astype(F32)
    both = (high + pltpu.roll(scale - high, SUM_HIGH, 1)).astype(BF16)
    shape = (LANES, width)
    k, column = iota(shape, 0), iota(shape, 1)
    spread = one_hot(((k & (SUM_HIGH - 1)) == column // HD) & (k < 2 * SUM_HIGH))
    return dot(both, spread)


def merged(first, second, width):
    a, b = first[:, width:].astype(F32), second[:, width:].astype(F32)
    valid = iota((1, LANES), 1) < H
    top = jnp.maximum(a, b)
    scale_a = jnp.where(valid, jnp.exp(a - top), 0.0)
    scale_b = jnp.where(valid, jnp.exp(b - top), 0.0)

    def total(s):
        return pltpu.roll(s, LANES - SUM_HIGH, 1) + pltpu.roll(s, LANES - SUM_LOW, 1)

    return top, total(a) * scale_a + total(b) * scale_b, scale_a, scale_b, valid


def join_kernel(at_ref, own_ref, other_ref, keep_ref, send_ref):
    half, total_width = own_ref.shape
    width = total_width - LANES
    rows = half // 2
    for ref, which in ((send_ref, 1 - at_ref[0]), (keep_ref, at_ref[0])):
        pick = pl.ds(pl.multiple_of(which * rows, 16), rows)
        first, second = own_ref[pick, :], other_ref[pick, :]
        top, total, scale_a, scale_b, valid = merged(first, second, width)
        ref[:, :width] = (
            first[:, :width].astype(F32) * expanded(scale_a, width)
            + second[:, :width].astype(F32) * expanded(scale_b, width)
        ).astype(BF16)
        high = total.astype(BF16).astype(F32)
        stat = jnp.where(valid, top, 0.0)
        stat = stat + pltpu.roll(jnp.where(valid, high, 0.0), SUM_HIGH, 1)
        stat = stat + pltpu.roll(jnp.where(valid, total - high, 0.0), SUM_LOW, 1)
        ref[:, width:] = stat.astype(BF16)


def project_kernel(at_ref, own_ref, other_ref, w0, w1, w2, w3, residual_ref, gain_ref, normed_ref, out_ref, attended):
    rows, total_width = own_ref.shape
    width = total_width - LANES
    first, second = own_ref[...], other_ref[...]
    _, total, scale_a, scale_b, valid = merged(first, second, width)
    inverse = 1.0 / jnp.where(valid, total, 1.0)
    attended[...] = (
        first[:, :width].astype(F32) * expanded(scale_a * inverse, width)
        + second[:, :width].astype(F32) * expanded(scale_b * inverse, width)
    ).astype(BF16)
    mixed = None
    depth = w0.shape[0]
    for flip, weight in enumerate((w0, w1, w2, w3)):
        column = pl.multiple_of((at_ref[0] ^ flip) * depth, LANES)
        term = dot(attended[:, pl.ds(column, depth)], weight[...])
        mixed = term if mixed is None else mixed + term
    residual = (residual_ref[...].astype(F32) + mixed).astype(BF16)
    out_ref[...] = residual
    wide = residual.astype(F32)
    scale = lax.rsqrt(jnp.mean(wide * wide, axis=-1, keepdims=True) + 1e-05)
    normed_ref[...] = (wide * scale * gain_ref[...]).astype(BF16)


def feed_kernel(main, tail, x0, x1, x2, x3, weight_ref, down_ref, keep_ref, send_ref):
    x = jnp.concatenate([x0[...], x1[...], x2[...], x3[...]], 0)
    sums = dot(x, weight_ref[...])

    def silu(v):
        return v / (1.0 + jnp.exp(-v))

    lane = iota((1, LANES), 1)
    end = sums[:, 2 * main :]
    last = silu(end) * pltpu.roll(end, LANES - tail, 1)
    hidden = jnp.concatenate(
        [
            (silu(sums[:, :main]) * sums[:, main : 2 * main]).astype(BF16),
            jnp.where(lane < tail, last, 0.0).astype(BF16),
        ],
        1,
    )
    out = dot(hidden, down_ref[...]).astype(BF16)
    half = out.shape[0] // 2
    keep_ref[...] = out[:half]
    send_ref[...] = out[half:]


def feed(main, tail, parts, weight, down):
    rows, width = parts[0].shape
    half = jax.ShapeDtypeStruct((2 * rows, width), BF16)
    return pl.pallas_call(
        functools.partial(feed_kernel, main, tail),
        in_specs=[VMEM] * 6,
        out_specs=[VMEM] * 2,
        out_shape=[half, half],
        compiler_params=params(),
        cost_estimate=pl.CostEstimate(
            flops=2 * 4 * rows * width * 1408, bytes_accessed=6 * 1024 * 1024, transcendentals=4 * rows * main
        ),
        name="feed",
    )(*parts, weight, down)


def per_device(
    residual_in,
    queries,
    key_cache,
    value_cache,
    cache_lengths,
    out_weight,
    norm_gain,
    gate_weight,
    up_weight,
    down_weight,
):
    dp_size, kv_size = lax.axis_size("dp"), lax.axis_size("kv")
    inner = dp_size // OUTER
    dp_index, kv_index = lax.axis_index("dp"), lax.axis_index("kv")
    z, y = dp_index // inner, dp_index % inner
    units = gate_weight.shape[1]
    main = units // OUTER // LANES * LANES
    tail = units // OUTER - main
    width = residual_in.shape[1]

    def kv_flip(a, bit):
        return lax.ppermute(a, "kv", [(i, i ^ bit) for i in range(kv_size)])

    def z_shift(a, by):
        return lax.ppermute(a, "dp", [(i, (i + by * inner) % dp_size) for i in range(dp_size)])

    def y_flip(a, bit):
        return lax.ppermute(a, "dp", [(i, i ^ bit) for i in range(dp_size)])

    rows = gate_weight.shape[0]
    columns = down_weight.shape[1]
    packed = pl.pallas_call(
        functools.partial(pack_kernel, main, tail),
        in_specs=[SMEM] + [VMEM] * 3,
        out_specs=[VMEM] * (2 * OUTER),
        out_shape=[jax.ShapeDtypeStruct((rows, 2 * main + LANES), BF16)] * OUTER
        + [jax.ShapeDtypeStruct((main // 2 + tail, 2 * columns), BF16)] * OUTER,
        compiler_params=params(),
        name="pack",
    )(z.reshape(1), gate_weight, up_weight, down_weight)

    gate_up = [packed[0]] + [z_shift(packed[s], s) for s in range(1, OUTER)]
    downs = [packed[OUTER]] + [z_shift(packed[OUTER + s], s) for s in range(1, OUTER)]

    def shared(block, axis, folded):
        bit = 1
        while 2 * bit < inner:
            other = y_flip(block, bit)
            upper = (y & bit) > 0
            low, high = jnp.where(upper, other, block), jnp.where(upper, block, other)
            if folded:
                size = low.shape[1] // 2
                block = jnp.concatenate([low[:, :size], high[:, :size], low[:, size:], high[:, size:]], 1)
            else:
                block = jnp.concatenate([low, high], 0)
            bit *= 2
        return [block, y_flip(block, bit)]

    gate_up = [part for block in gate_up for part in shared(block, 0, False)]
    downs = [part for block in downs for part in shared(block, 1, True)]
    unit_rows = (main + tail + LANES - 1) // LANES * LANES
    weight, down = pl.pallas_call(
        functools.partial(unpack_kernel, main, tail),
        in_specs=[SMEM] + [VMEM] * (4 * OUTER),
        out_specs=[VMEM] * 2,
        out_shape=[
            jax.ShapeDtypeStruct((width, 2 * main + LANES), BF16),
            jax.ShapeDtypeStruct((unit_rows, width), BF16),
        ],
        compiler_params=params(),
        name="unpack",
    )(jnp.stack([z, (y >= inner // 2).astype(jnp.int32)]), *gate_up, *downs)

    core, chip = kv_index % 2, kv_index // 2
    at = jnp.concatenate([jnp.stack([kv_index * key_cache.shape[1], core]), cache_lengths])
    keep, send = attention(queries, key_cache, value_cache, at)
    other = kv_flip(send, 1)
    half = jax.ShapeDtypeStruct((keep.shape[0] // 2, keep.shape[1]), BF16)
    keep, send = pl.pallas_call(
        join_kernel,
        in_specs=[SMEM, VMEM, VMEM],
        out_specs=[VMEM, VMEM],
        out_shape=[half, half],
        compiler_params=params(),
        name="join",
    )(chip.reshape(1), keep, other)
    other = kv_flip(send, 2)
    w1, w2 = kv_flip(out_weight, 1), kv_flip(out_weight, 2)
    w3 = kv_flip(w2, 1)
    tokens = jax.ShapeDtypeStruct(residual_in.shape, BF16)
    normed, residual = pl.pallas_call(
        project_kernel,
        in_specs=[SMEM] + [VMEM] * 8,
        out_specs=[VMEM, VMEM],
        out_shape=[tokens, tokens],
        scratch_shapes=[pltpu.VMEM(residual_in.shape, BF16)],
        compiler_params=params(),
        name="project",
    )(kv_index.reshape(1), keep, other, out_weight, w1, w2, w3, residual_in, norm_gain.reshape(1, width))

    def added(a, b):
        return (a.astype(F32) + b.astype(F32)).astype(BF16)

    mlp = None
    for shift in (0, 1, 3, 2):
        here = normed if shift == 0 else z_shift(normed, shift)
        there = kv_flip(here, 2)
        parts = [here, there, kv_flip(here, 1), kv_flip(there, 1)]
        keep, send = feed(main, tail, parts, weight, down)
        both = added(keep, kv_flip(send, 1))
        count = residual_in.shape[0]
        term = added(both[:count], kv_flip(both[count:], 2))
        if shift:
            term = z_shift(term, -shift)
        term = term.astype(F32)
        mlp = term if mlp is None else mlp + term
    return (residual.astype(F32) + mlp).astype(BF16)


def solution(mesh):
    placed = (
        P(("dp", "kv"), None),
        P("dp", None),
        P("dp", "kv", None),
        P("dp", "kv", None),
        P("dp"),
        P("kv", None),
        P(),
        P("dp", "kv"),
        P("dp", "kv"),
        P("kv", "dp"),
    )
    return jax.shard_map(
        per_device, mesh=mesh, in_specs=placed, out_specs=P(("dp", "kv"), None), check_vma=False
    )
```

```python
import functools

import jax
import jax.numpy as jnp
from jax import lax
from jax.experimental import pallas as pl
from jax.experimental.pallas import tpu as pltpu
from jax.sharding import PartitionSpec as P

H = 24
HD = 64
KVH = 8
LANES = 128
SUM_HIGH = 32
SUM_LOW = 64
OUTER = 4

VMEM = pl.BlockSpec(memory_space=pltpu.VMEM)
SMEM = pl.BlockSpec(memory_space=pltpu.SMEM)
HBM = pl.BlockSpec(memory_space=pl.ANY)
NT = (((1,), (1,)), ((), ()))
BF16 = jnp.bfloat16
F32 = jnp.float32


def params(mib):
    return pltpu.CompilerParams(vmem_limit_bytes=mib * 1024 * 1024)


def iota(shape, dim):
    return lax.broadcasted_iota(jnp.int32, shape, dim)


def dot(a, b):
    return jnp.dot(a, b, preferred_element_type=F32)


def one_hot(condition):
    return jnp.where(condition, 1.0, 0.0).astype(BF16)


def pack_kernel(main, tail, cuts, z_ref, gate_ref, up_ref, down_ref, *refs):
    outs, slots, (weights, sems, in_sems) = refs[: len(cuts)], refs[len(cuts) : -3], refs[-3:]
    tail_at = OUTER * main
    total = weights.shape[1]
    step = total // 2 if total % 32 == 0 else total
    loads = []
    for index, ref in enumerate((gate_ref, up_ref, down_ref)):
        for start in range(0, total, step):
            pick = pl.ds(start, step)
            loads.append(pltpu.make_async_copy(ref.at[pick], weights.at[index, pick], in_sems.at[len(loads)]))
            loads[-1].start()
    for load in loads:
        load.wait()
    gate_ref, up_ref, down_ref = (weights.at[index] for index in range(3))
    second = 2 * main + LANES
    copies = []
    for index, (shift, start, rows) in enumerate(cuts):
        out = slots[index]
        target = z_ref[0] ^ shift
        pick = slice(start, start + rows)
        column = pl.multiple_of(target * main, LANES)
        out[:, :main] = gate_ref[pick, pl.ds(column, main)]
        out[:, main : 2 * main] = up_ref[pick, pl.ds(column, main)]
        out[:, second : second + main] = down_ref[pick, pl.ds(column, main)]
        shape = (OUTER * tail, LANES)
        k, lane = iota(shape, 0) - target * tail, iota(shape, 1)
        first = one_hot((lane < tail) & (k == lane))
        next_to = one_hot((lane >= tail) & (lane < 2 * tail) & (k == lane - tail))
        ends = dot(gate_ref[pick, tail_at:], first) + dot(up_ref[pick, tail_at:], next_to)
        out[:, 2 * main : second] = ends.astype(BF16)
        out[:, second + main :] = dot(down_ref[pick, tail_at:], first).astype(BF16)
        copies.append(pltpu.make_async_copy(out, outs[index], sems.at[index]))
        copies[-1].start()
    for copy in copies:
        copy.wait()


def place_kernel(spots, at_ref, *refs):
    blocks, out = refs[:-1], refs[-1]
    for block, (start, step, mine) in zip(blocks, spots):
        side = at_ref[0] if mine else 1 - at_ref[0]
        out[pl.ds(pl.multiple_of(start + step * side, 16), block.shape[0]), :] = block[...]


def place(blocks, spots, at):
    rows = sum(block.shape[0] for block in blocks)
    return pl.pallas_call(
        functools.partial(place_kernel, spots),
        in_specs=[SMEM] + [VMEM] * len(blocks),
        out_specs=VMEM,
        out_shape=jax.ShapeDtypeStruct((rows, blocks[0].shape[1]), BF16),
        compiler_params=params(16),
        name="place",
    )(at, *blocks)


def attention_kernel(at_ref, q_hbm, k_hbm, v_hbm, keep_ref, send_ref, q_ref, k_ref, v_ref, bias, result, stats, lines, sems):
    rows, width = q_ref.shape
    requests, slab, _ = k_ref.shape
    block = 2 * (H // KVH) * HD
    steps = width // block
    span = rows - (requests - 1)
    heads = block // HD
    group = H // KVH
    first_key, half_row = at_ref[0], at_ref[1]

    def load(source, target, index):
        return pltpu.make_async_copy(source, target, sems.at[index])

    loads = [load(q_hbm, q_ref, 0)]
    loads += [load(k_hbm.at[r], k_ref.at[r], 1 + r) for r in range(requests)]
    loads += [load(v_hbm.at[r], v_ref.at[r], 1 + requests + r) for r in range(requests)]
    order = [0, 1, 1 + requests] + [i for i in range(2, len(loads)) if i != 1 + requests]
    for index in order:
        loads[index].start()

    place = first_key + iota((slab, rows), 0)
    limit = at_ref[2] - span + iota((slab, rows), 1)
    bias[...] = jnp.where(place <= limit, 0.0, -1e30)
    stats[...] = jnp.zeros_like(stats)
    lines[...] = jnp.zeros_like(lines)

    lane = iota((1, LANES), 1)
    low_lanes = lane < HD

    def in_half(a):
        return low_lanes if a == 0 else ~low_lanes

    def placed(value, h):
        return pltpu.roll(value, HD, 1) if h % 2 != h // group else value

    def record(old, column, top, total):
        high = total.astype(BF16).astype(F32)
        old = jnp.where(lane == column, top, old)
        old = jnp.where(lane == column + SUM_HIGH, high, old)
        return jnp.where(lane == column + SUM_LOW, total - high, old)

    for index in order[:3]:
        loads[index].wait()

    def one(step):
        near = pl.ds(step * LANES, LANES)

        def aligned(h):
            column = step * block + h // 2 * LANES
            tile = placed(q_ref[:, pl.ds(column, LANES)].astype(F32) * HD**-0.5, h)
            return jnp.where(in_half(h // group), tile, 0.0)

        keys, value = k_ref[0, :, near], v_ref[0, :, near]
        stat = stats[...]
        queries = [aligned(h) for h in range(heads)]
        sub = iota((8, 1), 0)
        for r in range(1, requests):
            line = jnp.zeros((8, LANES), F32)
            for h in range(heads):
                last = queries[h][rows - 8 :][8 - requests + r : 9 - requests + r]
                line = jnp.where(sub == h, jnp.broadcast_to(last, (8, LANES)), line)
            lines[r - 1, pl.ds(step * 8, 8), near] = line
        outs = []
        for a in range(2):
            query = jnp.concatenate(queries[a * group : (a + 1) * group], 0).astype(BF16)
            scores = lax.dot_general(keys, query, NT, preferred_element_type=F32)
            scores = scores + jnp.concatenate([bias[...]] * group, 1)
            top = jnp.maximum(jnp.max(scores, axis=0, keepdims=True), -1e29).astype(BF16).astype(F32)
            weights = jnp.exp((scores - top).astype(BF16))
            values = jnp.where(in_half(a), value, jnp.ones((), BF16)).astype(F32).T.astype(BF16)
            out = dot(values, weights).T
            top = jnp.broadcast_to(top, (8, top.shape[1])).T[:, :1]
            total = jnp.where(in_half(a), pltpu.roll(out, HD, 1), out)
            for r in range(group):
                h = a * group + r
                pick = slice(r * rows, (r + 1) * rows)
                stat = record(stat, step * heads + h, top[pick], total[pick])
                outs.append(placed(out[pick], h))
                if h % 2 == 1:
                    column = step * block + h // 2 * LANES
                    result[:, pl.ds(column, LANES)] = jnp.where(low_lanes, outs[h - 1], outs[h])
        stats[...] = stat

    for step in range(steps):
        one(step)
    count = 8 * steps
    sub, column = iota((count, 1), 0), iota((1, LANES), 1)
    spot = sub // 8 * heads + sub % 8
    live = sub % 8 < heads
    for r in range(1, requests):
        loads[1 + r].wait()
        loads[1 + requests + r].wait()
        row = rows - requests + r
        scores = lax.dot_general(lines[r - 1].astype(BF16), k_ref[r], NT, preferred_element_type=F32)
        usable = first_key + iota((1, slab), 1) < at_ref[2 + r]
        scores = jnp.where(usable, scores, -1e30)
        top = jnp.maximum(jnp.max(scores, axis=1, keepdims=True), -1e29).astype(BF16).astype(F32)
        weights = jnp.exp(scores - top)
        total = jnp.sum(weights, axis=1, keepdims=True)
        out = dot(weights.astype(BF16), v_ref[r])
        high = total.astype(BF16).astype(F32)
        stat = jnp.where(live & (column == spot), top, 0.0)
        stat = stat + jnp.where(live & (column == spot + SUM_HIGH), high, 0.0)
        stat = stat + jnp.where(live & (column == spot + SUM_LOW), total - high, 0.0)
        stats[row : row + 1, :] = jnp.sum(stat, axis=0, keepdims=True)
        for step in range(steps):
            tile = out[8 * step : 8 * step + 8, step * LANES : (step + 1) * LANES]
            turned = pltpu.roll(tile, HD, 1)
            for h in range(0, heads, 2):
                low = (turned if h // group else tile)[h : h + 1]
                high = (tile if (h + 1) // group else turned)[h + 1 : h + 2]
                at = step * block + h // 2 * LANES
                result[row : row + 1, at : at + LANES] = jnp.where(low_lanes, low, high)

    quarter = rows // 4
    for ref, which in ((keep_ref, half_row), (send_ref, 1 - half_row)):
        for part in range(2):
            pick = pl.ds(pl.multiple_of((2 * part + which) * quarter, 16), quarter)
            ref[part * quarter : (part + 1) * quarter, :width] = result[pick, :].astype(BF16)
            ref[part * quarter : (part + 1) * quarter, width:] = stats[pick, :].astype(BF16)


def attention(queries, keys, values, at):
    rows, width = queries.shape
    requests, slab, depth = keys.shape
    half = jax.ShapeDtypeStruct((rows // 2, width + LANES), BF16)
    return pl.pallas_call(
        attention_kernel,
        in_specs=[SMEM, HBM, HBM, HBM],
        out_specs=[VMEM, VMEM],
        out_shape=[half, half],
        scratch_shapes=[
            pltpu.VMEM(queries.shape, BF16),
            pltpu.VMEM(keys.shape, BF16),
            pltpu.VMEM(values.shape, BF16),
            pltpu.VMEM((slab, rows), F32),
            pltpu.VMEM((rows, width), F32),
            pltpu.VMEM((rows, LANES), F32),
            pltpu.VMEM((requests - 1, 8 * width // (2 * (H // KVH) * HD), depth), F32),
            pltpu.SemaphoreType.DMA((1 + 2 * requests,)),
        ],
        compiler_params=params(56),
        name="attention",
    )(at, queries, keys, values)


def expanded(scale, width):
    high = scale.astype(BF16).astype(F32)
    both = (high + pltpu.roll(scale - high, SUM_HIGH, 1)).astype(BF16)
    shape = (LANES, width)
    k, column = iota(shape, 0), iota(shape, 1)
    spread = one_hot(((k & (SUM_HIGH - 1)) == column // HD) & (k < 2 * SUM_HIGH))
    return dot(both, spread)


def merged(parts, width):
    tiles = [part[:, width:].astype(F32) for part in parts]
    valid = iota((1, LANES), 1) < width // HD
    top = functools.reduce(jnp.maximum, tiles)
    scales = [jnp.where(valid, jnp.exp(tile - top), 0.0) for tile in tiles]
    sums = [pltpu.roll(tile, LANES - SUM_HIGH, 1) + pltpu.roll(tile, LANES - SUM_LOW, 1) for tile in tiles]
    total = functools.reduce(jnp.add, [a * b for a, b in zip(sums, scales)])
    return top, total, scales, valid


def weighted(parts, scales, width):
    terms = [part[:, :width].astype(F32) * expanded(scale, width) for part, scale in zip(parts, scales)]
    return functools.reduce(jnp.add, terms).astype(BF16)


def join_kernel(at_ref, own_ref, other_ref, keep_ref, send_ref):
    rows, width = keep_ref.shape[0], own_ref.shape[1] - LANES
    for ref, which in ((send_ref, 1 - at_ref[0]), (keep_ref, at_ref[0])):
        pick = pl.ds(pl.multiple_of(which * rows, 16), rows)
        parts = [own_ref[pick, :], other_ref[pick, :]]
        top, total, scales, valid = merged(parts, width)
        ref[:, :width] = weighted(parts, scales, width)
        high = total.astype(BF16).astype(F32)
        stat = jnp.where(valid, top, 0.0)
        stat = stat + pltpu.roll(jnp.where(valid, high, 0.0), SUM_HIGH, 1)
        stat = stat + pltpu.roll(jnp.where(valid, total - high, 0.0), SUM_LOW, 1)
        ref[:, width:] = stat.astype(BF16)


def project_kernel(at_ref, own_ref, other_ref, w0, w1, w2, w3, residual_ref, gain_ref, normed_ref, out_ref, attended):
    width = own_ref.shape[1] - LANES
    parts = [own_ref[...], other_ref[...]]
    _, total, scales, valid = merged(parts, width)
    inverse = 1.0 / jnp.where(valid, total, 1.0)
    attended[...] = weighted(parts, [scale * inverse for scale in scales], width)
    mixed = None
    depth = w0.shape[0]
    for flip, weight in enumerate((w0, w1, w2, w3)):
        column = pl.multiple_of((at_ref[0] ^ flip) * depth, LANES)
        term = dot(attended[:, pl.ds(column, depth)], weight[...])
        mixed = term if mixed is None else mixed + term
    residual = (residual_ref[...].astype(F32) + mixed).astype(BF16)
    out_ref[...] = residual
    wide = residual.astype(F32)
    scale = lax.rsqrt(jnp.mean(wide * wide, axis=-1, keepdims=True) + 1e-05)
    normed_ref[...] = (wide * scale * gain_ref[...]).astype(BF16)


def feed_kernel(main, tail, count, order, z_ref, *refs):
    tokens, weights = refs[:count], refs[count : count + 4]
    keep_ref, send_ref, x = refs[count + 4 :]
    width = x.shape[1]
    block = width // OUTER
    rows = tokens[0].shape[0]
    columns = [pl.multiple_of((z_ref[0] ^ b) * block, LANES) for b in order]
    for index, ref in enumerate(tokens):
        for b in range(OUTER):
            x[index * rows : (index + 1) * rows, b * block : (b + 1) * block] = ref[:, pl.ds(columns[b], block)]

    def silu(v):
        return v / (1.0 + jnp.exp(-v))

    lane = iota((1, LANES), 1)
    second = 2 * main + LANES
    depth = weights[0].shape[0]
    hidden = []
    for first, last in (weights[:2], weights[2:]):
        sums = dot(x[:, :depth], first[:, :second]) + dot(x[:, depth:], last[:, :second])
        end = sums[:, 2 * main :]
        ends = silu(end) * pltpu.roll(end, LANES - tail, 1)
        hidden.append(
            jnp.concatenate(
                [
                    (silu(sums[:, :main]) * sums[:, main : 2 * main]).astype(BF16),
                    jnp.where(lane < tail, ends, 0.0).astype(BF16),
                ],
                1,
            )
        )
    half = count * rows // 2
    for b in range(OUTER):
        place = b * block
        which = place // depth
        pick = slice(place - which * depth, place - which * depth + block)
        out = lax.dot_general(hidden[0], weights[which][pick, second:], NT, preferred_element_type=F32)
        out = out + lax.dot_general(hidden[1], weights[2 + which][pick, second:], NT, preferred_element_type=F32)
        out = out.astype(BF16)
        keep_ref[:, pl.ds(columns[b], block)] = out[:half]
        send_ref[:, pl.ds(columns[b], block)] = out[half:]


def feed(main, tail, order, z, tokens, weights):
    rows, width = tokens[0].shape
    count = len(tokens)
    half = jax.ShapeDtypeStruct((count * rows // 2, width), BF16)
    return pl.pallas_call(
        functools.partial(feed_kernel, main, tail, count, order),
        in_specs=[SMEM] + [VMEM] * (count + 4),
        out_specs=[VMEM] * 2,
        out_shape=[half, half],
        scratch_shapes=[pltpu.VMEM((count * rows, width), BF16)],
        compiler_params=params(24),
        name="feed",
    )(z, *tokens, *weights)


def after(value, *others):
    return lax.optimization_barrier((value, *others))[0]


def per_device(
    residual_in,
    queries,
    key_cache,
    value_cache,
    cache_lengths,
    out_weight,
    norm_gain,
    gate_weight,
    up_weight,
    down_weight,
):
    dp_size, kv_size = lax.axis_size("dp"), lax.axis_size("kv")
    inner = dp_size // OUTER
    dp_index, kv_index = lax.axis_index("dp"), lax.axis_index("kv")
    z, y = (dp_index // inner).reshape(1), dp_index % inner
    core, chip = kv_index % 2, kv_index // 2
    units = gate_weight.shape[1]
    main = units // OUTER // LANES * LANES
    tail = units // OUTER - main
    width = residual_in.shape[1]

    def kv_flip(a, bit):
        return lax.ppermute(a, "kv", [(i, i ^ bit) for i in range(kv_size)])

    def z_flip(a, by):
        return lax.ppermute(a, "dp", [(i, i ^ (by * inner)) for i in range(dp_size)])

    def y_flip(a, bit):
        return lax.ppermute(a, "dp", [(i, i ^ bit) for i in range(dp_size)])

    w2 = kv_flip(out_weight, 2)
    w1 = kv_flip(out_weight, 1)

    rows = gate_weight.shape[0]
    cuts = [(flip, 0, rows) for flip in range(OUTER)]
    sizes = [(size, 3 * main + 2 * LANES) for _, _, size in cuts]
    packed = pl.pallas_call(
        functools.partial(pack_kernel, main, tail, cuts),
        in_specs=[SMEM] + [HBM] * 3,
        out_specs=[HBM] * len(cuts),
        out_shape=[jax.ShapeDtypeStruct(size, BF16) for size in sizes],
        scratch_shapes=[pltpu.VMEM(size, BF16) for size in sizes]
        + [
            pltpu.VMEM((3,) + gate_weight.shape, BF16),
            pltpu.SemaphoreType.DMA((len(cuts),)),
            pltpu.SemaphoreType.DMA((6,)),
        ],
        compiler_params=params(60),
        name="pack",
    )(after(z, w1), gate_weight, up_weight, down_weight.T)

    def shared(block):
        bit = 1
        while 2 * bit < inner:
            other = y_flip(block, bit)
            upper = (y & bit) > 0
            block = jnp.concatenate([jnp.where(upper, other, block), jnp.where(upper, block, other)], 0)
            bit *= 2
        return [block, y_flip(block, bit)]

    y_place = (y >= inner // 2).astype(jnp.int32).reshape(1)

    arrived = {index: z_flip(packed[index], index) for index in (1, 2)}
    blocks = {0: shared(packed[0])}
    at = jnp.concatenate([jnp.stack([kv_index * key_cache.shape[1], core]), cache_lengths])
    keep, send = attention(queries, key_cache, value_cache, after(at, *packed))
    arrived[3] = z_flip(after(packed[3], keep), 3)
    blocks[1] = shared(after(arrived[1], keep))
    other = kv_flip(after(send, blocks[0][1], arrived[1]), 1)
    half = jax.ShapeDtypeStruct((keep.shape[0] // 2, keep.shape[1]), BF16)
    keep, send = pl.pallas_call(
        join_kernel,
        in_specs=[SMEM, VMEM, VMEM],
        out_specs=[VMEM, VMEM],
        out_shape=[half, half],
        compiler_params=params(16),
        name="join",
    )(after(chip.reshape(1), arrived[2]), keep, other)
    other = kv_flip(send, 2)
    blocks[2] = shared(after(arrived[2], keep))
    w3 = kv_flip(after(w2, keep), 1)
    tokens = jax.ShapeDtypeStruct(residual_in.shape, BF16)
    normed, residual = pl.pallas_call(
        project_kernel,
        in_specs=[SMEM] + [VMEM] * 8,
        out_specs=[VMEM, VMEM],
        out_shape=[tokens, tokens],
        scratch_shapes=[pltpu.VMEM(residual_in.shape, BF16)],
        compiler_params=params(16),
        name="project",
    )(after(kv_index.reshape(1), blocks[1][1]), keep, other, out_weight, w1, w2, w3, residual_in, norm_gain.reshape(1, width))
    blocks[3] = shared(after(arrived[3], normed))

    order = (0, 1, 2, 3)
    deep = width // OUTER

    def laid(indices, base, *others):
        spots, parts = [], []
        for index in indices:
            for mine in (True, False):
                spots.append((index * deep - base, deep // 2, mine))
                parts.append(blocks[index][0 if mine else 1])
        return place(parts, spots, after(y_place, *others))

    near = [laid((0, 1), 0, normed)]
    count = residual_in.shape[0]
    here = {s: z_flip(normed, s) if s else normed for s in order}
    there = {s: kv_flip(here[s], 2) for s in order}
    near.append(laid((2, 3), 2 * deep, there[0], here[1], here[2]))
    weights = near + [kv_flip(part, 1) for part in near]

    def added(a, b):
        return (a.astype(F32) + b.astype(F32)).astype(BF16)

    mlp = None
    for shifts in ((0,), (1,), (2,), (3,)):
        tokens = [here[s] for s in shifts] + [there[s] for s in shifts]
        keep, send = feed(main, tail, order, z, tokens, weights)
        other = kv_flip(send, 2)
        for index, s in enumerate(shifts):
            pick = slice(index * count, (index + 1) * count)
            term = added(keep[pick], other[pick])
            if s:
                term = z_flip(term, s)
            mlp = term.astype(F32) if mlp is None else mlp + term.astype(F32)
    return (residual.astype(F32) + mlp).astype(BF16)


def solution(mesh):
    placed = (
        P(("dp", "kv"), None),
        P("dp", None),
        P("dp", "kv", None),
        P("dp", "kv", None),
        P("dp"),
        P("kv", None),
        P(),
        P("dp", "kv"),
        P("dp", "kv"),
        P("kv", "dp"),
    )
    return jax.shard_map(
        per_device, mesh=mesh, in_specs=placed, out_specs=P(("dp", "kv"), None), check_vma=False
    )
```

```python
import functools

import jax
import jax.numpy as jnp
from jax import lax
from jax.experimental import pallas as pl
from jax.experimental.pallas import tpu as pltpu
from jax.sharding import PartitionSpec as P

H = 24
HD = 64
KVH = 8
LANES = 128
SUM_HIGH = 32
SUM_LOW = 64
OUTER = 4

VMEM = pl.BlockSpec(memory_space=pltpu.VMEM)
SMEM = pl.BlockSpec(memory_space=pltpu.SMEM)
HBM = pl.BlockSpec(memory_space=pl.ANY)
NT = (((1,), (1,)), ((), ()))
BF16 = jnp.bfloat16
F32 = jnp.float32


def params(mib):
    return pltpu.CompilerParams(vmem_limit_bytes=mib * 1024 * 1024)


def iota(shape, dim):
    return lax.broadcasted_iota(jnp.int32, shape, dim)


def dot(a, b):
    return jnp.dot(a, b, preferred_element_type=F32)


def one_hot(condition):
    return jnp.where(condition, 1.0, 0.0).astype(BF16)


def pack_kernel(main, tail, cuts, z_ref, gate_ref, up_ref, down_ref, *refs):
    outs, slots, (weights, sems, in_sems) = refs[: len(cuts)], refs[len(cuts) : -3], refs[-3:]
    tail_at = OUTER * main
    total = weights.shape[1]
    step = total // 2 if total % 32 == 0 else total
    loads = []
    for index, ref in enumerate((gate_ref, up_ref, down_ref)):
        for start in range(0, total, step):
            pick = pl.ds(start, step)
            loads.append(pltpu.make_async_copy(ref.at[pick], weights.at[index, pick], in_sems.at[len(loads)]))
            loads[-1].start()
    for load in loads:
        load.wait()
    gate_ref, up_ref, down_ref = (weights.at[index] for index in range(3))
    second = 2 * main + LANES
    copies = []
    for index, (shift, start, rows) in enumerate(cuts):
        out = slots[index]
        target = z_ref[0] ^ shift
        pick = slice(start, start + rows)
        column = pl.multiple_of(target * main, LANES)
        out[:, :main] = gate_ref[pick, pl.ds(column, main)]
        out[:, main : 2 * main] = up_ref[pick, pl.ds(column, main)]
        out[:, second : second + main] = down_ref[pick, pl.ds(column, main)]
        shape = (OUTER * tail, LANES)
        k, lane = iota(shape, 0) - target * tail, iota(shape, 1)
        first = one_hot((lane < tail) & (k == lane))
        next_to = one_hot((lane >= tail) & (lane < 2 * tail) & (k == lane - tail))
        ends = dot(gate_ref[pick, tail_at:], first) + dot(up_ref[pick, tail_at:], next_to)
        out[:, 2 * main : second] = ends.astype(BF16)
        out[:, second + main :] = dot(down_ref[pick, tail_at:], first).astype(BF16)
        copies.append(pltpu.make_async_copy(out, outs[index], sems.at[index]))
        copies[-1].start()
    for copy in copies:
        copy.wait()


def place_kernel(spots, at_ref, *refs):
    blocks, out = refs[:-1], refs[-1]
    for block, (start, step, mine) in zip(blocks, spots):
        side = at_ref[0] if mine else 1 - at_ref[0]
        out[pl.ds(pl.multiple_of(start + step * side, 16), block.shape[0]), :] = block[...]


def place(blocks, spots, at):
    rows = sum(block.shape[0] for block in blocks)
    return pl.pallas_call(
        functools.partial(place_kernel, spots),
        in_specs=[SMEM] + [VMEM] * len(blocks),
        out_specs=VMEM,
        out_shape=jax.ShapeDtypeStruct((rows, blocks[0].shape[1]), BF16),
        compiler_params=params(16),
        name="place",
    )(at, *blocks)


def attention_kernel(at_ref, lengths_ref, q_hbm, k_hbm, v_hbm, keep_ref, send_ref, q_ref, k_ref, v_ref, bias, result, stats, lines, sems):
    rows, width = q_ref.shape
    requests, slab, _ = k_ref.shape
    block = 2 * (H // KVH) * HD
    steps = width // block
    span = rows - (requests - 1)
    heads = block // HD
    group = H // KVH
    first_key, half_row = at_ref[0] * slab, lax.rem(at_ref[0], 2)

    def load(source, target, index):
        return pltpu.make_async_copy(source, target, sems.at[index])

    loads = [load(q_hbm, q_ref, 0)]
    loads += [load(k_hbm.at[r], k_ref.at[r], 1 + r) for r in range(requests)]
    loads += [load(v_hbm.at[r], v_ref.at[r], 1 + requests + r) for r in range(requests)]
    order = [0, 1, 1 + requests] + [i for i in range(2, len(loads)) if i != 1 + requests]
    for index in order:
        loads[index].start()

    place = first_key + iota((slab, rows), 0)
    limit = lengths_ref[0] - span + iota((slab, rows), 1)
    bias[...] = jnp.where(place <= limit, 0.0, -1e30)
    stats[...] = jnp.zeros_like(stats)
    lines[...] = jnp.zeros_like(lines)

    lane = iota((1, LANES), 1)
    low_lanes = lane < HD

    def in_half(a):
        return low_lanes if a == 0 else ~low_lanes

    def placed(value, h):
        return pltpu.roll(value, HD, 1) if h % 2 != h // group else value

    def record(old, column, top, total):
        high = total.astype(BF16).astype(F32)
        old = jnp.where(lane == column, top, old)
        old = jnp.where(lane == column + SUM_HIGH, high, old)
        return jnp.where(lane == column + SUM_LOW, total - high, old)

    for index in order[:3]:
        loads[index].wait()

    def one(step):
        near = pl.ds(step * LANES, LANES)

        def aligned(h):
            column = step * block + h // 2 * LANES
            tile = placed(q_ref[:, pl.ds(column, LANES)].astype(F32) * HD**-0.5, h)
            return jnp.where(in_half(h // group), tile, 0.0)

        keys, value = k_ref[0, :, near], v_ref[0, :, near]
        stat = stats[...]
        queries = [aligned(h) for h in range(heads)]
        sub = iota((8, 1), 0)
        for r in range(1, requests):
            line = jnp.zeros((8, LANES), F32)
            for h in range(heads):
                last = queries[h][rows - 8 :][8 - requests + r : 9 - requests + r]
                line = jnp.where(sub == h, jnp.broadcast_to(last, (8, LANES)), line)
            lines[r - 1, pl.ds(step * 8, 8), near] = line
        outs = []
        for a in range(2):
            query = jnp.concatenate(queries[a * group : (a + 1) * group], 0).astype(BF16)
            scores = lax.dot_general(keys, query, NT, preferred_element_type=F32)
            scores = scores + jnp.concatenate([bias[...]] * group, 1)
            top = jnp.maximum(jnp.max(scores, axis=0, keepdims=True), -1e29).astype(BF16).astype(F32)
            weights = jnp.exp((scores - top).astype(BF16))
            values = jnp.where(in_half(a), value, jnp.ones((), BF16)).astype(F32).T.astype(BF16)
            out = dot(values, weights).T
            top = jnp.broadcast_to(top, (8, top.shape[1])).T[:, :1]
            total = jnp.where(in_half(a), pltpu.roll(out, HD, 1), out)
            for r in range(group):
                h = a * group + r
                pick = slice(r * rows, (r + 1) * rows)
                stat = record(stat, step * heads + h, top[pick], total[pick])
                outs.append(placed(out[pick], h))
                if h % 2 == 1:
                    column = step * block + h // 2 * LANES
                    result[:, pl.ds(column, LANES)] = jnp.where(low_lanes, outs[h - 1], outs[h])
        stats[...] = stat

    for step in range(steps):
        one(step)
    count = 8 * steps
    sub, column = iota((count, 1), 0), iota((1, LANES), 1)
    spot = sub // 8 * heads + sub % 8
    live = sub % 8 < heads
    for r in range(1, requests):
        loads[1 + r].wait()
        loads[1 + requests + r].wait()
        row = rows - requests + r
        scores = lax.dot_general(lines[r - 1].astype(BF16), k_ref[r], NT, preferred_element_type=F32)
        usable = first_key + iota((1, slab), 1) < lengths_ref[r]
        scores = jnp.where(usable, scores, -1e30)
        top = jnp.maximum(jnp.max(scores, axis=1, keepdims=True), -1e29).astype(BF16).astype(F32)
        weights = jnp.exp(scores - top)
        total = jnp.sum(weights, axis=1, keepdims=True)
        out = dot(weights.astype(BF16), v_ref[r])
        high = total.astype(BF16).astype(F32)
        stat = jnp.where(live & (column == spot), top, 0.0)
        stat = stat + jnp.where(live & (column == spot + SUM_HIGH), high, 0.0)
        stat = stat + jnp.where(live & (column == spot + SUM_LOW), total - high, 0.0)
        stats[row : row + 1, :] = jnp.sum(stat, axis=0, keepdims=True)
        for step in range(steps):
            tile = out[8 * step : 8 * step + 8, step * LANES : (step + 1) * LANES]
            turned = pltpu.roll(tile, HD, 1)
            for h in range(0, heads, 2):
                low = (turned if h // group else tile)[h : h + 1]
                high = (tile if (h + 1) // group else turned)[h + 1 : h + 2]
                at = step * block + h // 2 * LANES
                result[row : row + 1, at : at + LANES] = jnp.where(low_lanes, low, high)

    quarter = rows // 4
    for ref, which in ((keep_ref, half_row), (send_ref, 1 - half_row)):
        for part in range(2):
            pick = pl.ds(pl.multiple_of((2 * part + which) * quarter, 16), quarter)
            ref[part * quarter : (part + 1) * quarter, :width] = result[pick, :].astype(BF16)
            ref[part * quarter : (part + 1) * quarter, width:] = stats[pick, :].astype(BF16)


def attention(queries, keys, values, at, lengths):
    rows, width = queries.shape
    requests, slab, depth = keys.shape
    half = jax.ShapeDtypeStruct((rows // 2, width + LANES), BF16)
    return pl.pallas_call(
        attention_kernel,
        in_specs=[SMEM, SMEM, HBM, HBM, HBM],
        out_specs=[VMEM, VMEM],
        out_shape=[half, half],
        scratch_shapes=[
            pltpu.VMEM(queries.shape, BF16),
            pltpu.VMEM(keys.shape, BF16),
            pltpu.VMEM(values.shape, BF16),
            pltpu.VMEM((slab, rows), F32),
            pltpu.VMEM((rows, width), F32),
            pltpu.VMEM((rows, LANES), F32),
            pltpu.VMEM((requests - 1, 8 * width // (2 * (H // KVH) * HD), depth), F32),
            pltpu.SemaphoreType.DMA((1 + 2 * requests,)),
        ],
        compiler_params=params(56),
        name="attention",
    )(at, lengths, queries, keys, values)


def expanded(scale, width):
    high = scale.astype(BF16).astype(F32)
    both = (high + pltpu.roll(scale - high, SUM_HIGH, 1)).astype(BF16)
    shape = (LANES, width)
    k, column = iota(shape, 0), iota(shape, 1)
    spread = one_hot(((k & (SUM_HIGH - 1)) == column // HD) & (k < 2 * SUM_HIGH))
    return dot(both, spread)


def merged(parts, width):
    tiles = [part[:, width:].astype(F32) for part in parts]
    valid = iota((1, LANES), 1) < width // HD
    top = functools.reduce(jnp.maximum, tiles)
    scales = [jnp.where(valid, jnp.exp(tile - top), 0.0) for tile in tiles]
    sums = [pltpu.roll(tile, LANES - SUM_HIGH, 1) + pltpu.roll(tile, LANES - SUM_LOW, 1) for tile in tiles]
    total = functools.reduce(jnp.add, [a * b for a, b in zip(sums, scales)])
    return top, total, scales, valid


def weighted(parts, scales, width):
    terms = [part[:, :width].astype(F32) * expanded(scale, width) for part, scale in zip(parts, scales)]
    return functools.reduce(jnp.add, terms).astype(BF16)


def join_kernel(at_ref, own_ref, other_ref, keep_ref, send_ref):
    width, part_width = own_ref.shape[1] - LANES, keep_ref.shape[1] - LANES
    own, other = own_ref[...], other_ref[...]
    top, total, scales, _ = merged([own, other], width)
    valid = iota((1, LANES), 1) < part_width // HD
    for ref, which in ((send_ref, 1 - at_ref[0]), (keep_ref, at_ref[0])):

        def here(tile):
            moved = pltpu.roll(tile, LANES - part_width // HD, 1)
            return jnp.where(valid, jnp.where(which == 1, moved, tile), 0.0)

        pick = pl.ds(pl.multiple_of(which * part_width, LANES), part_width)
        ref[:, :part_width] = weighted([own_ref[:, pick], other_ref[:, pick]], [here(scale) for scale in scales], part_width)
        sums = here(total)
        high = sums.astype(BF16).astype(F32)
        stat = here(top) + pltpu.roll(high, SUM_HIGH, 1) + pltpu.roll(sums - high, SUM_LOW, 1)
        ref[:, part_width:] = stat.astype(BF16)


def project_kernel(at_ref, own_ref, other_ref, w0, w1, keep_ref, send_ref, attended, mixed):
    width = own_ref.shape[1] - LANES
    parts = [own_ref[...], other_ref[...]]
    _, total, scales, valid = merged(parts, width)
    inverse = 1.0 / jnp.where(valid, total, 1.0)
    attended[...] = weighted(parts, [scale * inverse for scale in scales], width)
    depth = w0.shape[0]
    core, chip = lax.rem(at_ref[0], 2), at_ref[0] // 2
    first = dot(attended[:, pl.ds(pl.multiple_of(core * depth, LANES), depth)], w0[...])
    second = dot(attended[:, pl.ds(pl.multiple_of((1 - core) * depth, LANES), depth)], w1[...])
    mixed[...] = first + second
    rows = keep_ref.shape[0]
    keep_ref[...] = mixed[pl.ds(pl.multiple_of(chip * rows, 16), rows), :]
    send_ref[...] = mixed[pl.ds(pl.multiple_of((1 - chip) * rows, 16), rows), :].astype(BF16)


def norm_kernel(keep_ref, other_ref, residual_ref, gain_ref, normed_ref, out_ref):
    mixed = keep_ref[...] + other_ref[...].astype(F32)
    residual = (residual_ref[...].astype(F32) + mixed).astype(BF16)
    out_ref[...] = residual
    wide = residual.astype(F32)
    scale = lax.rsqrt(jnp.mean(wide * wide, axis=-1, keepdims=True) + 1e-05)
    normed_ref[...] = (wide * scale * gain_ref[...]).astype(BF16)


def feed_kernel(main, tail, count, order, z_ref, *refs):
    tokens, weights = refs[:count], refs[count : count + 4]
    keep_ref, send_ref, x = refs[count + 4 :]
    width = x.shape[1]
    block = width // OUTER
    rows = tokens[0].shape[0]
    columns = [pl.multiple_of((z_ref[0] ^ b) * block, LANES) for b in order]
    for index, ref in enumerate(tokens):
        for b in range(OUTER):
            x[index * rows : (index + 1) * rows, b * block : (b + 1) * block] = ref[:, pl.ds(columns[b], block)]

    def silu(v):
        return v / (1.0 + jnp.exp(-v))

    lane = iota((1, LANES), 1)
    second = 2 * main + LANES
    depth = weights[0].shape[0]
    hidden = []
    for first, last in (weights[:2], weights[2:]):
        sums = dot(x[:, :depth], first[:, :second]) + dot(x[:, depth:], last[:, :second])
        end = sums[:, 2 * main :]
        ends = silu(end) * pltpu.roll(end, LANES - tail, 1)
        hidden.append(
            jnp.concatenate(
                [
                    (silu(sums[:, :main]) * sums[:, main : 2 * main]).astype(BF16),
                    jnp.where(lane < tail, ends, 0.0).astype(BF16),
                ],
                1,
            )
        )
    half = count * rows // 2
    for b in range(OUTER):
        place = b * block
        which = place // depth
        pick = slice(place - which * depth, place - which * depth + block)
        out = lax.dot_general(hidden[0], weights[which][pick, second:], NT, preferred_element_type=F32)
        out = out + lax.dot_general(hidden[1], weights[2 + which][pick, second:], NT, preferred_element_type=F32)
        out = out.astype(BF16)
        keep_ref[:, pl.ds(columns[b], block)] = out[:half]
        send_ref[:, pl.ds(columns[b], block)] = out[half:]


def feed(main, tail, order, z, tokens, weights):
    rows, width = tokens[0].shape
    count = len(tokens)
    half = jax.ShapeDtypeStruct((count * rows // 2, width), BF16)
    return pl.pallas_call(
        functools.partial(feed_kernel, main, tail, count, order),
        in_specs=[SMEM] + [VMEM] * (count + 4),
        out_specs=[VMEM] * 2,
        out_shape=[half, half],
        scratch_shapes=[pltpu.VMEM((count * rows, width), BF16)],
        compiler_params=params(24),
        name="feed",
    )(z, *tokens, *weights)


def after(value, *others):
    return lax.optimization_barrier((value, *others))[0]


def per_device(
    residual_in,
    queries,
    key_cache,
    value_cache,
    cache_lengths,
    out_weight,
    norm_gain,
    gate_weight,
    up_weight,
    down_weight,
):
    dp_size, kv_size = lax.axis_size("dp"), lax.axis_size("kv")
    inner = dp_size // OUTER
    dp_index, kv_index = lax.axis_index("dp"), lax.axis_index("kv")
    z, y = (dp_index // inner).reshape(1), dp_index % inner
    chip = kv_index // 2
    units = gate_weight.shape[1]
    main = units // OUTER // LANES * LANES
    tail = units // OUTER - main
    width = residual_in.shape[1]

    def kv_flip(a, bit):
        return lax.ppermute(a, "kv", [(i, i ^ bit) for i in range(kv_size)])

    def z_flip(a, by):
        return lax.ppermute(a, "dp", [(i, i ^ (by * inner)) for i in range(dp_size)])

    def y_flip(a, bit):
        return lax.ppermute(a, "dp", [(i, i ^ bit) for i in range(dp_size)])

    rows = gate_weight.shape[0]
    cuts = [(flip, 0, rows) for flip in range(OUTER)]
    sizes = [(size, 3 * main + 2 * LANES) for _, _, size in cuts]
    packed = pl.pallas_call(
        functools.partial(pack_kernel, main, tail, cuts),
        in_specs=[SMEM] + [HBM] * 3,
        out_specs=[HBM] * len(cuts),
        out_shape=[jax.ShapeDtypeStruct(size, BF16) for size in sizes],
        scratch_shapes=[pltpu.VMEM(size, BF16) for size in sizes]
        + [
            pltpu.VMEM((3,) + gate_weight.shape, BF16),
            pltpu.SemaphoreType.DMA((len(cuts),)),
            pltpu.SemaphoreType.DMA((6,)),
        ],
        compiler_params=params(60),
        name="pack",
    )(z, gate_weight, up_weight, down_weight.T)

    def shared(block):
        bit = 1
        while 2 * bit < inner:
            other = y_flip(block, bit)
            upper = (y & bit) > 0
            block = jnp.concatenate([jnp.where(upper, other, block), jnp.where(upper, block, other)], 0)
            bit *= 2
        return [block, y_flip(block, bit)]

    y_place = (y >= inner // 2).astype(jnp.int32).reshape(1)

    arrived = {index: z_flip(packed[index], index) for index in (2, 1)}
    blocks = {0: shared(packed[0])}
    w1 = kv_flip(after(out_weight, packed[0]), 1)
    own = kv_index.reshape(1)
    keep, send = attention(queries, key_cache, value_cache, after(own, *packed), cache_lengths)
    arrived[3] = z_flip(after(packed[3], keep), 3)
    other = kv_flip(after(send, blocks[0][1], w1), 1)
    half = jax.ShapeDtypeStruct((keep.shape[0], width // 2 + LANES), BF16)
    keep, send = pl.pallas_call(
        join_kernel,
        in_specs=[SMEM, VMEM, VMEM],
        out_specs=[VMEM, VMEM],
        out_shape=[half, half],
        compiler_params=params(16),
        name="join",
    )(after(chip.reshape(1), arrived[1], arrived[2]), keep, other)
    other = kv_flip(send, 2)
    blocks[1] = shared(after(arrived[1], keep))
    blocks[2] = shared(after(arrived[2], keep))
    tokens = jax.ShapeDtypeStruct(residual_in.shape, BF16)
    partial, send = pl.pallas_call(
        project_kernel,
        in_specs=[SMEM] + [VMEM] * 4,
        out_specs=[VMEM, VMEM],
        out_shape=[jax.ShapeDtypeStruct(residual_in.shape, F32), tokens],
        scratch_shapes=[
            pltpu.VMEM((keep.shape[0], width // 2), BF16),
            pltpu.VMEM((keep.shape[0], width), F32),
        ],
        compiler_params=params(16),
        name="project",
    )(own, keep, other, out_weight, w1)
    other = kv_flip(send, 2)
    normed, residual = pl.pallas_call(
        norm_kernel,
        in_specs=[VMEM] * 4,
        out_specs=[VMEM, VMEM],
        out_shape=[tokens, tokens],
        compiler_params=params(16),
        name="norm",
    )(after(partial, blocks[1][1]), other, residual_in, norm_gain.reshape(1, width))

    order = (0, 1, 2, 3)
    deep = width // OUTER

    def laid(indices, base, *others):
        spots, parts = [], []
        for index in indices:
            for mine in (True, False):
                spots.append((index * deep - base, deep // 2, mine))
                parts.append(blocks[index][0 if mine else 1])
        return place(parts, spots, after(y_place, *others))

    near = [laid((0, 1), 0, normed)]
    count = residual_in.shape[0]
    here = {0: normed, 1: z_flip(normed, 1), 3: z_flip(normed, 3)}
    here[2] = z_flip(after(normed, here[3]), 2)
    there = {s: kv_flip(here[s], 2) for s in order}
    blocks[3] = shared(after(arrived[3], blocks[2][1], here[1]))
    near.append(laid((2, 3), 2 * deep, there[1], here[3]))
    weights = near + [kv_flip(part, 1) for part in near]

    def added(a, b):
        return (a.astype(F32) + b.astype(F32)).astype(BF16)

    mlp = residual.astype(F32)
    kept, arrivals, terms = [], [], []
    for s in (3, 1, 2, 0):
        turn = after(z, *kept[-1:], *arrivals[:-1], *terms[:-2])
        keep, send = feed(main, tail, order, turn, [here[s], there[s]], weights)
        other = kv_flip(send, 2)
        kept.append(keep)
        arrivals.append(other)
        term = added(keep, other)
        terms.append(z_flip(term, s) if s else term)
        mlp = mlp + terms[-1].astype(F32)
    return mlp.astype(BF16)


def solution(mesh):
    placed = (
        P(("dp", "kv"), None),
        P("dp", None),
        P("dp", "kv", None),
        P("dp", "kv", None),
        P("dp"),
        P("kv", None),
        P(),
        P("dp", "kv"),
        P("dp", "kv"),
        P("kv", "dp"),
    )
    return jax.shard_map(
        per_device, mesh=mesh, in_specs=placed, out_specs=P(("dp", "kv"), None), check_vma=False
    )
```

```python
import functools

import jax
import jax.numpy as jnp
from jax import lax
from jax.experimental import pallas as pl
from jax.experimental.pallas import tpu as pltpu
from jax.sharding import PartitionSpec as P

H = 24
HD = 64
KVH = 8
LANES = 128
SUM_HIGH = 32
SUM_LOW = 64
OUTER = 4

VMEM = pl.BlockSpec(memory_space=pltpu.VMEM)
SMEM = pl.BlockSpec(memory_space=pltpu.SMEM)
HBM = pl.BlockSpec(memory_space=pl.ANY)
NT = (((1,), (1,)), ((), ()))
BF16 = jnp.bfloat16
F32 = jnp.float32


def params(mib):
    return pltpu.CompilerParams(vmem_limit_bytes=mib * 1024 * 1024)


def iota(shape, dim):
    return lax.broadcasted_iota(jnp.int32, shape, dim)


def dot(a, b):
    return jnp.dot(a, b, preferred_element_type=F32)


def one_hot(condition):
    return jnp.where(condition, 1.0, 0.0).astype(BF16)


def pack_kernel(main, tail, cuts, z_ref, gate_ref, up_ref, down_ref, *refs):
    outs, slots, (weights, sems, in_sems) = refs[: len(cuts)], refs[len(cuts) : -3], refs[-3:]
    tail_at = OUTER * main
    total = weights.shape[1]
    step = total // 2 if total % 32 == 0 else total
    loads = []
    for index, ref in enumerate((gate_ref, up_ref, down_ref)):
        for start in range(0, total, step):
            pick = pl.ds(start, step)
            loads.append(pltpu.make_async_copy(ref.at[pick], weights.at[index, pick], in_sems.at[len(loads)]))
            loads[-1].start()
    for load in loads:
        load.wait()
    gate_ref, up_ref, down_ref = (weights.at[index] for index in range(3))
    second = 2 * main + LANES
    copies = []
    for index, (shift, start, rows) in enumerate(cuts):
        out = slots[index]
        target = z_ref[0] ^ shift
        pick = slice(start, start + rows)
        column = pl.multiple_of(target * main, LANES)
        out[:, :main] = gate_ref[pick, pl.ds(column, main)]
        out[:, main : 2 * main] = up_ref[pick, pl.ds(column, main)]
        out[:, second : second + main] = down_ref[pick, pl.ds(column, main)]
        shape = (OUTER * tail, LANES)
        k, lane = iota(shape, 0) - target * tail, iota(shape, 1)
        first = one_hot((lane < tail) & (k == lane))
        next_to = one_hot((lane >= tail) & (lane < 2 * tail) & (k == lane - tail))
        ends = dot(gate_ref[pick, tail_at:], first) + dot(up_ref[pick, tail_at:], next_to)
        out[:, 2 * main : second] = ends.astype(BF16)
        out[:, second + main :] = dot(down_ref[pick, tail_at:], first).astype(BF16)
        copies.append(pltpu.make_async_copy(out, outs[index], sems.at[index]))
        copies[-1].start()
    for copy in copies:
        copy.wait()


def place_kernel(spots, at_ref, *refs):
    blocks, out = refs[:-1], refs[-1]
    for block, (start, step, mine) in zip(blocks, spots):
        side = at_ref[0] if mine else 1 - at_ref[0]
        out[pl.ds(pl.multiple_of(start + step * side, 16), block.shape[0]), :] = block[...]


def place(blocks, spots, at):
    rows = sum(block.shape[0] for block in blocks)
    return pl.pallas_call(
        functools.partial(place_kernel, spots),
        in_specs=[SMEM] + [VMEM] * len(blocks),
        out_specs=VMEM,
        out_shape=jax.ShapeDtypeStruct((rows, blocks[0].shape[1]), BF16),
        compiler_params=params(16),
        name="place",
    )(at, *blocks)


def attention_kernel(at_ref, lengths_ref, q_hbm, k_hbm, v_hbm, keep_ref, send_ref, q_ref, k_ref, v_ref, bias, result, stats, lines, sems):
    rows, width = q_ref.shape
    requests, slab, _ = k_ref.shape
    block = 2 * (H // KVH) * HD
    steps = width // block
    span = rows - (requests - 1)
    heads = block // HD
    group = H // KVH
    first_key, half_row = at_ref[0] * slab, lax.rem(at_ref[0], 2)

    def load(source, target, index):
        return pltpu.make_async_copy(source, target, sems.at[index])

    loads = [load(q_hbm, q_ref, 0)]
    loads += [load(k_hbm.at[r], k_ref.at[r], 1 + r) for r in range(requests)]
    loads += [load(v_hbm.at[r], v_ref.at[r], 1 + requests + r) for r in range(requests)]
    order = [0, 1, 1 + requests] + [i for i in range(2, len(loads)) if i != 1 + requests]
    for index in order:
        loads[index].start()

    place = first_key + iota((slab, rows), 0)
    limit = lengths_ref[0] - span + iota((slab, rows), 1)
    bias[...] = jnp.where(place <= limit, 0.0, -1e30)
    stats[...] = jnp.zeros_like(stats)
    lines[...] = jnp.zeros_like(lines)

    lane = iota((1, LANES), 1)
    low_lanes = lane < HD

    def in_half(a):
        return low_lanes if a == 0 else ~low_lanes

    def placed(value, h):
        return pltpu.roll(value, HD, 1) if h % 2 != h // group else value

    def record(old, column, top, total):
        high = total.astype(BF16).astype(F32)
        old = jnp.where(lane == column, top, old)
        old = jnp.where(lane == column + SUM_HIGH, high, old)
        return jnp.where(lane == column + SUM_LOW, total - high, old)

    for index in order[:3]:
        loads[index].wait()

    def one(step):
        near = pl.ds(step * LANES, LANES)

        def aligned(h):
            column = step * block + h // 2 * LANES
            tile = placed(q_ref[:, pl.ds(column, LANES)].astype(F32) * HD**-0.5, h)
            return jnp.where(in_half(h // group), tile, 0.0)

        keys, value = k_ref[0, :, near], v_ref[0, :, near]
        stat = stats[...]
        queries = [aligned(h) for h in range(heads)]
        sub = iota((8, 1), 0)
        for r in range(1, requests):
            line = jnp.zeros((8, LANES), F32)
            for h in range(heads):
                last = queries[h][rows - 8 :][8 - requests + r : 9 - requests + r]
                line = jnp.where(sub == h, jnp.broadcast_to(last, (8, LANES)), line)
            lines[r - 1, pl.ds(step * 8, 8), near] = line
        outs = []
        for a in range(2):
            query = jnp.concatenate(queries[a * group : (a + 1) * group], 0).astype(BF16)
            scores = lax.dot_general(keys, query, NT, preferred_element_type=F32)
            scores = scores + jnp.concatenate([bias[...]] * group, 1)
            top = jnp.maximum(jnp.max(scores, axis=0, keepdims=True), -1e29).astype(BF16).astype(F32)
            weights = jnp.exp((scores - top).astype(BF16))
            values = jnp.where(in_half(a), value, jnp.ones((), BF16)).astype(F32).T.astype(BF16)
            out = dot(values, weights).T
            top = jnp.broadcast_to(top, (8, top.shape[1])).T[:, :1]
            total = jnp.where(in_half(a), pltpu.roll(out, HD, 1), out)
            for r in range(group):
                h = a * group + r
                pick = slice(r * rows, (r + 1) * rows)
                stat = record(stat, step * heads + h, top[pick], total[pick])
                outs.append(placed(out[pick], h))
                if h % 2 == 1:
                    column = step * block + h // 2 * LANES
                    result[:, pl.ds(column, LANES)] = jnp.where(low_lanes, outs[h - 1], outs[h])
        stats[...] = stat

    for step in range(steps):
        one(step)
    count = 8 * steps
    sub, column = iota((count, 1), 0), iota((1, LANES), 1)
    spot = sub // 8 * heads + sub % 8
    live = sub % 8 < heads
    for r in range(1, requests):
        loads[1 + r].wait()
        loads[1 + requests + r].wait()
        row = rows - requests + r
        scores = lax.dot_general(lines[r - 1].astype(BF16), k_ref[r], NT, preferred_element_type=F32)
        usable = first_key + iota((1, slab), 1) < lengths_ref[r]
        scores = jnp.where(usable, scores, -1e30)
        top = jnp.maximum(jnp.max(scores, axis=1, keepdims=True), -1e29).astype(BF16).astype(F32)
        weights = jnp.exp(scores - top)
        total = jnp.sum(weights, axis=1, keepdims=True)
        out = dot(weights.astype(BF16), v_ref[r])
        high = total.astype(BF16).astype(F32)
        stat = jnp.where(live & (column == spot), top, 0.0)
        stat = stat + jnp.where(live & (column == spot + SUM_HIGH), high, 0.0)
        stat = stat + jnp.where(live & (column == spot + SUM_LOW), total - high, 0.0)
        stats[row : row + 1, :] = jnp.sum(stat, axis=0, keepdims=True)
        for step in range(steps):
            tile = out[8 * step : 8 * step + 8, step * LANES : (step + 1) * LANES]
            turned = pltpu.roll(tile, HD, 1)
            for h in range(0, heads, 2):
                low = (turned if h // group else tile)[h : h + 1]
                high = (tile if (h + 1) // group else turned)[h + 1 : h + 2]
                at = step * block + h // 2 * LANES
                result[row : row + 1, at : at + LANES] = jnp.where(low_lanes, low, high)

    quarter = rows // 4
    for ref, which in ((keep_ref, half_row), (send_ref, 1 - half_row)):
        for part in range(2):
            pick = pl.ds(pl.multiple_of((2 * part + which) * quarter, 16), quarter)
            ref[part * quarter : (part + 1) * quarter, :width] = result[pick, :].astype(BF16)
            ref[part * quarter : (part + 1) * quarter, width:] = stats[pick, :].astype(BF16)


def attention(queries, keys, values, at, lengths):
    rows, width = queries.shape
    requests, slab, depth = keys.shape
    half = jax.ShapeDtypeStruct((rows // 2, width + LANES), BF16)
    return pl.pallas_call(
        attention_kernel,
        in_specs=[SMEM, SMEM, HBM, HBM, HBM],
        out_specs=[VMEM, VMEM],
        out_shape=[half, half],
        scratch_shapes=[
            pltpu.VMEM(queries.shape, BF16),
            pltpu.VMEM(keys.shape, BF16),
            pltpu.VMEM(values.shape, BF16),
            pltpu.VMEM((slab, rows), F32),
            pltpu.VMEM((rows, width), F32),
            pltpu.VMEM((rows, LANES), F32),
            pltpu.VMEM((requests - 1, 8 * width // (2 * (H // KVH) * HD), depth), F32),
            pltpu.SemaphoreType.DMA((1 + 2 * requests,)),
        ],
        compiler_params=params(56),
        name="attention",
    )(at, lengths, queries, keys, values)


def expanded(scale, width):
    high = scale.astype(BF16).astype(F32)
    both = (high + pltpu.roll(scale - high, SUM_HIGH, 1)).astype(BF16)
    shape = (LANES, width)
    k, column = iota(shape, 0), iota(shape, 1)
    spread = one_hot(((k & (SUM_HIGH - 1)) == column // HD) & (k < 2 * SUM_HIGH))
    return dot(both, spread)


def merged(parts, width):
    tiles = [part[:, width:].astype(F32) for part in parts]
    valid = iota((1, LANES), 1) < width // HD
    top = functools.reduce(jnp.maximum, tiles)
    scales = [jnp.where(valid, jnp.exp(tile - top), 0.0) for tile in tiles]
    sums = [pltpu.roll(tile, LANES - SUM_HIGH, 1) + pltpu.roll(tile, LANES - SUM_LOW, 1) for tile in tiles]
    total = functools.reduce(jnp.add, [a * b for a, b in zip(sums, scales)])
    return top, total, scales, valid


def weighted(parts, scales, width):
    terms = [part[:, :width].astype(F32) * expanded(scale, width) for part, scale in zip(parts, scales)]
    return functools.reduce(jnp.add, terms).astype(BF16)


def join_kernel(at_ref, own_ref, other_ref, keep_ref, send_ref):
    width, part_width = own_ref.shape[1] - LANES, keep_ref.shape[1] - LANES
    own, other = own_ref[...], other_ref[...]
    top, total, scales, _ = merged([own, other], width)
    valid = iota((1, LANES), 1) < part_width // HD
    for ref, which in ((send_ref, 1 - at_ref[0]), (keep_ref, at_ref[0])):

        def here(tile):
            moved = pltpu.roll(tile, LANES - part_width // HD, 1)
            return jnp.where(valid, jnp.where(which == 1, moved, tile), 0.0)

        pick = pl.ds(pl.multiple_of(which * part_width, LANES), part_width)
        ref[:, :part_width] = weighted([own_ref[:, pick], other_ref[:, pick]], [here(scale) for scale in scales], part_width)
        sums = here(total)
        high = sums.astype(BF16).astype(F32)
        stat = here(top) + pltpu.roll(high, SUM_HIGH, 1) + pltpu.roll(sums - high, SUM_LOW, 1)
        ref[:, part_width:] = stat.astype(BF16)


def project_kernel(at_ref, own_ref, other_ref, w0, w1, keep_ref, send_ref, attended, mixed):
    width = own_ref.shape[1] - LANES
    parts = [own_ref[...], other_ref[...]]
    _, total, scales, valid = merged(parts, width)
    inverse = 1.0 / jnp.where(valid, total, 1.0)
    attended[...] = weighted(parts, [scale * inverse for scale in scales], width)
    depth = w0.shape[0]
    core, chip = lax.rem(at_ref[0], 2), at_ref[0] // 2
    first = dot(attended[:, pl.ds(pl.multiple_of(core * depth, LANES), depth)], w0[...])
    second = dot(attended[:, pl.ds(pl.multiple_of((1 - core) * depth, LANES), depth)], w1[...])
    mixed[...] = first + second
    rows = keep_ref.shape[0]
    keep_ref[...] = mixed[pl.ds(pl.multiple_of(chip * rows, 16), rows), :]
    send_ref[...] = mixed[pl.ds(pl.multiple_of((1 - chip) * rows, 16), rows), :].astype(BF16)


def norm_kernel(keep_ref, other_ref, residual_ref, gain_ref, normed_ref, out_ref):
    mixed = keep_ref[...] + other_ref[...].astype(F32)
    residual = (residual_ref[...].astype(F32) + mixed).astype(BF16)
    out_ref[...] = residual
    wide = residual.astype(F32)
    scale = lax.rsqrt(jnp.mean(wide * wide, axis=-1, keepdims=True) + 1e-05)
    normed_ref[...] = (wide * scale * gain_ref[...]).astype(BF16)


def feed_kernel(main, tail, count, order, z_ref, *refs):
    tokens, weights = refs[:count], refs[count : count + 4]
    keep_ref, send_ref, x = refs[count + 4 :]
    width = x.shape[1]
    block = width // OUTER
    rows = tokens[0].shape[0]
    columns = [pl.multiple_of((z_ref[0] ^ b) * block, LANES) for b in order]
    for index, ref in enumerate(tokens):
        for b in range(OUTER):
            x[index * rows : (index + 1) * rows, b * block : (b + 1) * block] = ref[:, pl.ds(columns[b], block)]

    def silu(v):
        return v / (1.0 + jnp.exp(-v))

    lane = iota((1, LANES), 1)
    second = 2 * main + LANES
    depth = weights[0].shape[0]
    hidden = []
    for first, last in (weights[:2], weights[2:]):
        sums = dot(x[:, :depth], first[:, :second]) + dot(x[:, depth:], last[:, :second])
        end = sums[:, 2 * main :]
        ends = silu(end) * pltpu.roll(end, LANES - tail, 1)
        hidden.append(
            jnp.concatenate(
                [
                    (silu(sums[:, :main]) * sums[:, main : 2 * main]).astype(BF16),
                    jnp.where(lane < tail, ends, 0.0).astype(BF16),
                ],
                1,
            )
        )
    half = count * rows // 2
    for b in range(OUTER):
        place = b * block
        which = place // depth
        pick = slice(place - which * depth, place - which * depth + block)
        out = lax.dot_general(hidden[0], weights[which][pick, second:], NT, preferred_element_type=F32)
        out = out + lax.dot_general(hidden[1], weights[2 + which][pick, second:], NT, preferred_element_type=F32)
        out = out.astype(BF16)
        keep_ref[:, pl.ds(columns[b], block)] = out[:half]
        send_ref[:, pl.ds(columns[b], block)] = out[half:]


def feed(main, tail, order, z, tokens, weights):
    rows, width = tokens[0].shape
    count = len(tokens)
    half = jax.ShapeDtypeStruct((count * rows // 2, width), BF16)
    return pl.pallas_call(
        functools.partial(feed_kernel, main, tail, count, order),
        in_specs=[SMEM] + [VMEM] * (count + 4),
        out_specs=[VMEM] * 2,
        out_shape=[half, half],
        scratch_shapes=[pltpu.VMEM((count * rows, width), BF16)],
        compiler_params=params(24),
        name="feed",
    )(z, *tokens, *weights)


def after(value, *others):
    return lax.optimization_barrier((value, *others))[0]


def per_device(
    residual_in,
    queries,
    key_cache,
    value_cache,
    cache_lengths,
    out_weight,
    norm_gain,
    gate_weight,
    up_weight,
    down_weight,
):
    dp_size, kv_size = lax.axis_size("dp"), lax.axis_size("kv")
    inner = dp_size // OUTER
    dp_index, kv_index = lax.axis_index("dp"), lax.axis_index("kv")
    z, y = (dp_index // inner).reshape(1), dp_index % inner
    chip = kv_index // 2
    units = gate_weight.shape[1]
    main = units // OUTER // LANES * LANES
    tail = units // OUTER - main
    width = residual_in.shape[1]

    def kv_flip(a, bit):
        return lax.ppermute(a, "kv", [(i, i ^ bit) for i in range(kv_size)])

    def z_flip(a, by):
        return lax.ppermute(a, "dp", [(i, i ^ (by * inner)) for i in range(dp_size)])

    def y_flip(a, bit):
        return lax.ppermute(a, "dp", [(i, i ^ bit) for i in range(dp_size)])

    rows = gate_weight.shape[0]
    cuts = [(flip, 0, rows) for flip in range(OUTER)]
    sizes = [(size, 3 * main + 2 * LANES) for _, _, size in cuts]
    packed = pl.pallas_call(
        functools.partial(pack_kernel, main, tail, cuts),
        in_specs=[SMEM] + [HBM] * 3,
        out_specs=[HBM] * len(cuts),
        out_shape=[jax.ShapeDtypeStruct(size, BF16) for size in sizes],
        scratch_shapes=[pltpu.VMEM(size, BF16) for size in sizes]
        + [
            pltpu.VMEM((3,) + gate_weight.shape, BF16),
            pltpu.SemaphoreType.DMA((len(cuts),)),
            pltpu.SemaphoreType.DMA((6,)),
        ],
        compiler_params=params(60),
        name="pack",
    )(z, gate_weight, up_weight, down_weight.T)

    def shared(block):
        bit = 1
        while 2 * bit < inner:
            other = y_flip(block, bit)
            upper = (y & bit) > 0
            block = jnp.concatenate([jnp.where(upper, other, block), jnp.where(upper, block, other)], 0)
            bit *= 2
        return [block, y_flip(block, bit)]

    y_place = (y >= inner // 2).astype(jnp.int32).reshape(1)

    arrived = {index: z_flip(packed[index], index) for index in (2, 1)}
    blocks = {0: shared(packed[0])}
    w1 = kv_flip(after(out_weight, packed[0]), 1)
    own = kv_index.reshape(1)
    keep, send = attention(queries, key_cache, value_cache, after(own, *packed), cache_lengths)
    arrived[3] = z_flip(after(packed[3], arrived[2]), 3)
    other = kv_flip(send, 1)
    half = jax.ShapeDtypeStruct((keep.shape[0], width // 2 + LANES), BF16)
    keep, send = pl.pallas_call(
        join_kernel,
        in_specs=[SMEM, VMEM, VMEM],
        out_specs=[VMEM, VMEM],
        out_shape=[half, half],
        compiler_params=params(60),
        name="join",
    )(after(chip.reshape(1), arrived[2], arrived[1], blocks[0][1], w1), keep, other)
    other = kv_flip(send, 2)
    blocks[1] = shared(after(arrived[1], keep))
    blocks[2] = shared(after(arrived[2], keep))
    tokens = jax.ShapeDtypeStruct(residual_in.shape, BF16)
    partial, send = pl.pallas_call(
        project_kernel,
        in_specs=[SMEM] + [VMEM] * 4,
        out_specs=[VMEM, VMEM],
        out_shape=[jax.ShapeDtypeStruct(residual_in.shape, F32), tokens],
        scratch_shapes=[
            pltpu.VMEM((keep.shape[0], width // 2), BF16),
            pltpu.VMEM((keep.shape[0], width), F32),
        ],
        compiler_params=params(16),
        name="project",
    )(own, keep, other, out_weight, w1)
    other = kv_flip(send, 2)
    normed, residual = pl.pallas_call(
        norm_kernel,
        in_specs=[VMEM] * 4,
        out_specs=[VMEM, VMEM],
        out_shape=[tokens, tokens],
        compiler_params=params(60),
        name="norm",
    )(after(partial, arrived[3]), other, residual_in, norm_gain.reshape(1, width))

    order = (0, 1, 2, 3)
    deep = width // OUTER

    def laid(indices, base, *others):
        spots, parts = [], []
        for index in indices:
            for mine in (True, False):
                spots.append((index * deep - base, deep // 2, mine))
                parts.append(blocks[index][0 if mine else 1])
        return place(parts, spots, after(y_place, *others))

    near = [laid((0, 1), 0, normed)]
    count = residual_in.shape[0]
    here = {0: normed, 1: z_flip(normed, 1), 3: z_flip(normed, 3)}
    here[2] = z_flip(after(normed, here[1]), 2)
    there = {s: kv_flip(here[s], 2) for s in order}
    blocks[3] = shared(after(arrived[3], blocks[2][1]))
    near.append(laid((2, 3), 2 * deep, there[0], there[1], here[3]))
    weights = near + [kv_flip(part, 1) for part in near]

    def added(a, b):
        return (a.astype(F32) + b.astype(F32)).astype(BF16)

    mlp = residual.astype(F32)
    kept, arrivals, terms = [], [], []
    for s in (3, 1, 2, 0):
        turn = after(z, *kept[-1:], *arrivals[:-1], *terms[:-2])
        keep, send = feed(main, tail, order, turn, [here[s], there[s]], weights)
        other = kv_flip(send, 2)
        kept.append(keep)
        arrivals.append(other)
        term = added(keep, other)
        terms.append(z_flip(term, s) if s else term)
        mlp = mlp + terms[-1].astype(F32)
    return mlp.astype(BF16)


def solution(mesh):
    placed = (
        P(("dp", "kv"), None),
        P("dp", None),
        P("dp", "kv", None),
        P("dp", "kv", None),
        P("dp"),
        P("kv", None),
        P(),
        P("dp", "kv"),
        P("dp", "kv"),
        P("kv", "dp"),
    )
    return jax.shard_map(
        per_device, mesh=mesh, in_specs=placed, out_specs=P(("dp", "kv"), None), check_vma=False
    )
```

```python
import functools

import jax
import jax.numpy as jnp
from jax import lax
from jax.experimental import pallas as pl
from jax.experimental.pallas import tpu as pltpu
from jax.sharding import PartitionSpec as P

H = 24
HD = 64
KVH = 8
LANES = 128
SUM_HIGH = 32
SUM_LOW = 64
OUTER = 4

VMEM = pl.BlockSpec(memory_space=pltpu.VMEM)
SMEM = pl.BlockSpec(memory_space=pltpu.SMEM)
HBM = pl.BlockSpec(memory_space=pl.ANY)
NT = (((1,), (1,)), ((), ()))
BF16 = jnp.bfloat16
F32 = jnp.float32


def params(mib):
    return pltpu.CompilerParams(vmem_limit_bytes=mib * 1024 * 1024)


def iota(shape, dim):
    return lax.broadcasted_iota(jnp.int32, shape, dim)


def dot(a, b):
    return jnp.dot(a, b, preferred_element_type=F32)


def one_hot(condition):
    return jnp.where(condition, 1.0, 0.0).astype(BF16)


def pack_kernel(main, tail, cuts, z_ref, gate_ref, up_ref, down_ref, *refs):
    outs, slots, (weights, sems, in_sems) = refs[: len(cuts)], refs[len(cuts) : -3], refs[-3:]
    tail_at = OUTER * main
    total = weights.shape[1]
    step = total // 2 if total % 32 == 0 else total
    loads = []
    for index, ref in enumerate((gate_ref, up_ref, down_ref)):
        for start in range(0, total, step):
            pick = pl.ds(start, step)
            loads.append(pltpu.make_async_copy(ref.at[pick], weights.at[index, pick], in_sems.at[len(loads)]))
            loads[-1].start()
    for load in loads:
        load.wait()
    gate_ref, up_ref, down_ref = (weights.at[index] for index in range(3))
    second = 2 * main + LANES
    copies = []
    for index, (shift, start, rows) in enumerate(cuts):
        out = slots[index]
        target = z_ref[0] ^ shift
        pick = slice(start, start + rows)
        column = pl.multiple_of(target * main, LANES)
        out[:, :main] = gate_ref[pick, pl.ds(column, main)]
        out[:, main : 2 * main] = up_ref[pick, pl.ds(column, main)]
        out[:, second : second + main] = down_ref[pick, pl.ds(column, main)]
        shape = (OUTER * tail, LANES)
        k, lane = iota(shape, 0) - target * tail, iota(shape, 1)
        first = one_hot((lane < tail) & (k == lane))
        next_to = one_hot((lane >= tail) & (lane < 2 * tail) & (k == lane - tail))
        ends = dot(gate_ref[pick, tail_at:], first) + dot(up_ref[pick, tail_at:], next_to)
        out[:, 2 * main : second] = ends.astype(BF16)
        out[:, second + main :] = dot(down_ref[pick, tail_at:], first).astype(BF16)
        copies.append(pltpu.make_async_copy(out, outs[index], sems.at[index]))
        copies[-1].start()
    for copy in copies:
        copy.wait()


def place_kernel(spots, at_ref, *refs):
    blocks, out = refs[:-1], refs[-1]
    for block, (start, step, mine) in zip(blocks, spots):
        side = at_ref[0] if mine else 1 - at_ref[0]
        out[pl.ds(pl.multiple_of(start + step * side, 16), block.shape[0]), :] = block[...]


def place(blocks, spots, at):
    rows = sum(block.shape[0] for block in blocks)
    return pl.pallas_call(
        functools.partial(place_kernel, spots),
        in_specs=[SMEM] + [VMEM] * len(blocks),
        out_specs=VMEM,
        out_shape=jax.ShapeDtypeStruct((rows, blocks[0].shape[1]), BF16),
        compiler_params=params(16),
        name="place",
    )(at, *blocks)


def attention_kernel(at_ref, lengths_ref, q_hbm, k_hbm, v_hbm, keep_ref, send_ref, q_ref, k_ref, v_ref, bias, result, stats, lines, sems):
    rows, width = q_ref.shape
    requests, slab, _ = k_ref.shape
    block = 2 * (H // KVH) * HD
    steps = width // block
    span = rows - (requests - 1)
    heads = block // HD
    group = H // KVH
    first_key, half_row = at_ref[0] * slab, lax.rem(at_ref[0], 2)

    def load(source, target, index):
        return pltpu.make_async_copy(source, target, sems.at[index])

    loads = [load(q_hbm, q_ref, 0)]
    loads += [load(k_hbm.at[r], k_ref.at[r], 1 + r) for r in range(requests)]
    loads += [load(v_hbm.at[r], v_ref.at[r], 1 + requests + r) for r in range(requests)]
    order = [0, 1, 1 + requests] + [i for i in range(2, len(loads)) if i != 1 + requests]
    for index in order:
        loads[index].start()

    place = first_key + iota((slab, rows), 0)
    limit = lengths_ref[0] - span + iota((slab, rows), 1)
    bias[...] = jnp.where(place <= limit, 0.0, -1e30)
    stats[...] = jnp.zeros_like(stats)
    lines[...] = jnp.zeros_like(lines)

    lane = iota((1, LANES), 1)
    low_lanes = lane < HD

    def in_half(a):
        return low_lanes if a == 0 else ~low_lanes

    def placed(value, h):
        return pltpu.roll(value, HD, 1) if h % 2 != h // group else value

    def record(old, column, top, total):
        high = total.astype(BF16).astype(F32)
        old = jnp.where(lane == column, top, old)
        old = jnp.where(lane == column + SUM_HIGH, high, old)
        return jnp.where(lane == column + SUM_LOW, total - high, old)

    for index in order[:3]:
        loads[index].wait()

    def one(step):
        near = pl.ds(step * LANES, LANES)

        def aligned(h):
            column = step * block + h // 2 * LANES
            tile = placed(q_ref[:, pl.ds(column, LANES)].astype(F32) * HD**-0.5, h)
            return jnp.where(in_half(h // group), tile, 0.0)

        keys, value = k_ref[0, :, near], v_ref[0, :, near]
        stat = stats[...]
        queries = [aligned(h) for h in range(heads)]
        sub = iota((8, 1), 0)
        for r in range(1, requests):
            line = jnp.zeros((8, LANES), F32)
            for h in range(heads):
                last = queries[h][rows - 8 :][8 - requests + r : 9 - requests + r]
                line = jnp.where(sub == h, jnp.broadcast_to(last, (8, LANES)), line)
            lines[r - 1, pl.ds(step * 8, 8), near] = line
        outs = []
        for a in range(2):
            query = jnp.concatenate(queries[a * group : (a + 1) * group], 0).astype(BF16)
            scores = lax.dot_general(keys, query, NT, preferred_element_type=F32)
            scores = scores + jnp.concatenate([bias[...]] * group, 1)
            top = jnp.maximum(jnp.max(scores, axis=0, keepdims=True), -1e29).astype(BF16).astype(F32)
            weights = jnp.exp((scores - top).astype(BF16))
            values = jnp.where(in_half(a), value, jnp.ones((), BF16)).astype(F32).T.astype(BF16)
            out = dot(values, weights).T
            top = jnp.broadcast_to(top, (8, top.shape[1])).T[:, :1]
            total = jnp.where(in_half(a), pltpu.roll(out, HD, 1), out)
            for r in range(group):
                h = a * group + r
                pick = slice(r * rows, (r + 1) * rows)
                stat = record(stat, step * heads + h, top[pick], total[pick])
                outs.append(placed(out[pick], h))
                if h % 2 == 1:
                    column = step * block + h // 2 * LANES
                    result[:, pl.ds(column, LANES)] = jnp.where(low_lanes, outs[h - 1], outs[h])
        stats[...] = stat

    for step in range(steps):
        one(step)
    count = 8 * steps
    sub, column = iota((count, 1), 0), iota((1, LANES), 1)
    spot = sub // 8 * heads + sub % 8
    live = sub % 8 < heads
    for r in range(1, requests):
        loads[1 + r].wait()
        loads[1 + requests + r].wait()
        row = rows - requests + r
        scores = lax.dot_general(lines[r - 1].astype(BF16), k_ref[r], NT, preferred_element_type=F32)
        usable = first_key + iota((1, slab), 1) < lengths_ref[r]
        scores = jnp.where(usable, scores, -1e30)
        top = jnp.maximum(jnp.max(scores, axis=1, keepdims=True), -1e29).astype(BF16).astype(F32)
        weights = jnp.exp(scores - top)
        total = jnp.sum(weights, axis=1, keepdims=True)
        out = dot(weights.astype(BF16), v_ref[r])
        high = total.astype(BF16).astype(F32)
        stat = jnp.where(live & (column == spot), top, 0.0)
        stat = stat + jnp.where(live & (column == spot + SUM_HIGH), high, 0.0)
        stat = stat + jnp.where(live & (column == spot + SUM_LOW), total - high, 0.0)
        stats[row : row + 1, :] = jnp.sum(stat, axis=0, keepdims=True)
        for step in range(steps):
            tile = out[8 * step : 8 * step + 8, step * LANES : (step + 1) * LANES]
            turned = pltpu.roll(tile, HD, 1)
            for h in range(0, heads, 2):
                low = (turned if h // group else tile)[h : h + 1]
                high = (tile if (h + 1) // group else turned)[h + 1 : h + 2]
                at = step * block + h // 2 * LANES
                result[row : row + 1, at : at + LANES] = jnp.where(low_lanes, low, high)

    quarter = rows // 4
    for ref, which in ((keep_ref, half_row), (send_ref, 1 - half_row)):
        for part in range(2):
            pick = pl.ds(pl.multiple_of((2 * part + which) * quarter, 16), quarter)
            ref[part * quarter : (part + 1) * quarter, :width] = result[pick, :].astype(BF16)
            ref[part * quarter : (part + 1) * quarter, width:] = stats[pick, :].astype(BF16)


def attention(queries, keys, values, at, lengths):
    rows, width = queries.shape
    requests, slab, depth = keys.shape
    half = jax.ShapeDtypeStruct((rows // 2, width + LANES), BF16)
    return pl.pallas_call(
        attention_kernel,
        in_specs=[SMEM, SMEM, HBM, HBM, HBM],
        out_specs=[VMEM, VMEM],
        out_shape=[half, half],
        scratch_shapes=[
            pltpu.VMEM(queries.shape, BF16),
            pltpu.VMEM(keys.shape, BF16),
            pltpu.VMEM(values.shape, BF16),
            pltpu.VMEM((slab, rows), F32),
            pltpu.VMEM((rows, width), F32),
            pltpu.VMEM((rows, LANES), F32),
            pltpu.VMEM((requests - 1, 8 * width // (2 * (H // KVH) * HD), depth), F32),
            pltpu.SemaphoreType.DMA((1 + 2 * requests,)),
        ],
        compiler_params=params(56),
        name="attention",
    )(at, lengths, queries, keys, values)


def expanded(scale, width):
    high = scale.astype(BF16).astype(F32)
    both = (high + pltpu.roll(scale - high, SUM_HIGH, 1)).astype(BF16)
    shape = (LANES, width)
    k, column = iota(shape, 0), iota(shape, 1)
    spread = one_hot(((k & (SUM_HIGH - 1)) == column // HD) & (k < 2 * SUM_HIGH))
    return dot(both, spread)


def merged(parts, width):
    tiles = [part[:, width:].astype(F32) for part in parts]
    valid = iota((1, LANES), 1) < width // HD
    top = functools.reduce(jnp.maximum, tiles)
    scales = [jnp.where(valid, jnp.exp(tile - top), 0.0) for tile in tiles]
    sums = [pltpu.roll(tile, LANES - SUM_HIGH, 1) + pltpu.roll(tile, LANES - SUM_LOW, 1) for tile in tiles]
    total = functools.reduce(jnp.add, [a * b for a, b in zip(sums, scales)])
    return top, total, scales, valid


def weighted(parts, scales, width):
    terms = [part[:, :width].astype(F32) * expanded(scale, width) for part, scale in zip(parts, scales)]
    return functools.reduce(jnp.add, terms).astype(BF16)


def join_kernel(at_ref, own_ref, other_ref, keep_ref, send_ref):
    width, part_width = own_ref.shape[1] - LANES, keep_ref.shape[1] - LANES
    own, other = own_ref[...], other_ref[...]
    top, total, scales, _ = merged([own, other], width)
    valid = iota((1, LANES), 1) < part_width // HD
    for ref, which in ((send_ref, 1 - at_ref[0]), (keep_ref, at_ref[0])):

        def here(tile):
            moved = pltpu.roll(tile, LANES - part_width // HD, 1)
            return jnp.where(valid, jnp.where(which == 1, moved, tile), 0.0)

        pick = pl.ds(pl.multiple_of(which * part_width, LANES), part_width)
        ref[:, :part_width] = weighted([own_ref[:, pick], other_ref[:, pick]], [here(scale) for scale in scales], part_width)
        sums = here(total)
        high = sums.astype(BF16).astype(F32)
        stat = here(top) + pltpu.roll(high, SUM_HIGH, 1) + pltpu.roll(sums - high, SUM_LOW, 1)
        ref[:, part_width:] = stat.astype(BF16)


def project_kernel(at_ref, own_ref, other_ref, w0, w1, keep_ref, send_ref, attended, mixed):
    width = own_ref.shape[1] - LANES
    parts = [own_ref[...], other_ref[...]]
    _, total, scales, valid = merged(parts, width)
    inverse = 1.0 / jnp.where(valid, total, 1.0)
    attended[...] = weighted(parts, [scale * inverse for scale in scales], width)
    depth = w0.shape[0]
    core, chip = lax.rem(at_ref[0], 2), at_ref[0] // 2
    first = dot(attended[:, pl.ds(pl.multiple_of(core * depth, LANES), depth)], w0[...])
    second = dot(attended[:, pl.ds(pl.multiple_of((1 - core) * depth, LANES), depth)], w1[...])
    mixed[...] = first + second
    rows = keep_ref.shape[0]
    keep_ref[...] = mixed[pl.ds(pl.multiple_of(chip * rows, 16), rows), :]
    send_ref[...] = mixed[pl.ds(pl.multiple_of((1 - chip) * rows, 16), rows), :].astype(BF16)


def norm_kernel(keep_ref, other_ref, residual_ref, gain_ref, normed_ref, out_ref):
    mixed = keep_ref[...] + other_ref[...].astype(F32)
    residual = (residual_ref[...].astype(F32) + mixed).astype(BF16)
    out_ref[...] = residual
    wide = residual.astype(F32)
    scale = lax.rsqrt(jnp.mean(wide * wide, axis=-1, keepdims=True) + 1e-05)
    normed_ref[...] = (wide * scale * gain_ref[...]).astype(BF16)


def feed_kernel(main, tail, count, order, z_ref, *refs):
    tokens, weights = refs[:count], refs[count : count + 4]
    keep_ref, send_ref, x = refs[count + 4 :]
    width = x.shape[1]
    block = width // OUTER
    rows = tokens[0].shape[0]
    columns = [pl.multiple_of((z_ref[0] ^ b) * block, LANES) for b in order]
    for index, ref in enumerate(tokens):
        for b in range(OUTER):
            x[index * rows : (index + 1) * rows, b * block : (b + 1) * block] = ref[:, pl.ds(columns[b], block)]

    def silu(v):
        return v / (1.0 + jnp.exp(-v))

    lane = iota((1, LANES), 1)
    second = 2 * main + LANES
    depth = weights[0].shape[0]
    hidden = []
    for first, last in (weights[:2], weights[2:]):
        sums = dot(x[:, :depth], first[:, :second]) + dot(x[:, depth:], last[:, :second])
        end = sums[:, 2 * main :]
        ends = silu(end) * pltpu.roll(end, LANES - tail, 1)
        hidden.append(
            jnp.concatenate(
                [
                    (silu(sums[:, :main]) * sums[:, main : 2 * main]).astype(BF16),
                    jnp.where(lane < tail, ends, 0.0).astype(BF16),
                ],
                1,
            )
        )
    half = count * rows // 2
    for b in range(OUTER):
        place = b * block
        which = place // depth
        pick = slice(place - which * depth, place - which * depth + block)
        out = lax.dot_general(hidden[0], weights[which][pick, second:], NT, preferred_element_type=F32)
        out = out + lax.dot_general(hidden[1], weights[2 + which][pick, second:], NT, preferred_element_type=F32)
        out = out.astype(BF16)
        keep_ref[:, pl.ds(columns[b], block)] = out[:half]
        send_ref[:, pl.ds(columns[b], block)] = out[half:]


def feed(main, tail, order, z, tokens, weights):
    rows, width = tokens[0].shape
    count = len(tokens)
    half = jax.ShapeDtypeStruct((count * rows // 2, width), BF16)
    return pl.pallas_call(
        functools.partial(feed_kernel, main, tail, count, order),
        in_specs=[SMEM] + [VMEM] * (count + 4),
        out_specs=[VMEM] * 2,
        out_shape=[half, half],
        scratch_shapes=[pltpu.VMEM((count * rows, width), BF16)],
        compiler_params=params(24),
        name="feed",
    )(z, *tokens, *weights)


def after(value, *others):
    return lax.optimization_barrier((value, *others))[0]


def per_device(
    residual_in,
    queries,
    key_cache,
    value_cache,
    cache_lengths,
    out_weight,
    norm_gain,
    gate_weight,
    up_weight,
    down_weight,
):
    dp_size, kv_size = lax.axis_size("dp"), lax.axis_size("kv")
    inner = dp_size // OUTER
    dp_index, kv_index = lax.axis_index("dp"), lax.axis_index("kv")
    z, y = (dp_index // inner).reshape(1), dp_index % inner
    chip = kv_index // 2
    units = gate_weight.shape[1]
    main = units // OUTER // LANES * LANES
    tail = units // OUTER - main
    width = residual_in.shape[1]

    def kv_flip(a, bit):
        return lax.ppermute(a, "kv", [(i, i ^ bit) for i in range(kv_size)])

    def z_flip(a, by):
        return lax.ppermute(a, "dp", [(i, i ^ (by * inner)) for i in range(dp_size)])

    def y_flip(a, bit):
        return lax.ppermute(a, "dp", [(i, i ^ bit) for i in range(dp_size)])

    rows = gate_weight.shape[0]
    cuts = [(flip, 0, rows) for flip in range(OUTER)]
    sizes = [(size, 3 * main + 2 * LANES) for _, _, size in cuts]
    packed = pl.pallas_call(
        functools.partial(pack_kernel, main, tail, cuts),
        in_specs=[SMEM] + [HBM] * 3,
        out_specs=[HBM] * len(cuts),
        out_shape=[jax.ShapeDtypeStruct(size, BF16) for size in sizes],
        scratch_shapes=[pltpu.VMEM(size, BF16) for size in sizes]
        + [
            pltpu.VMEM((3,) + gate_weight.shape, BF16),
            pltpu.SemaphoreType.DMA((len(cuts),)),
            pltpu.SemaphoreType.DMA((6,)),
        ],
        compiler_params=params(60),
        name="pack",
    )(z, gate_weight, up_weight, down_weight.T)

    def shared(block):
        bit = 1
        while 2 * bit < inner:
            other = y_flip(block, bit)
            upper = (y & bit) > 0
            block = jnp.concatenate([jnp.where(upper, other, block), jnp.where(upper, block, other)], 0)
            bit *= 2
        return [block, y_flip(block, bit)]

    y_place = (y >= inner // 2).astype(jnp.int32).reshape(1)

    arrived = {index: z_flip(packed[index], index) for index in (2, 1)}
    blocks = {0: shared(packed[0])}
    w1 = kv_flip(after(out_weight, packed[0]), 1)
    own = kv_index.reshape(1)
    keep, send = attention(queries, key_cache, value_cache, after(own, *packed), cache_lengths)
    arrived[3] = z_flip(after(packed[3], arrived[2]), 3)
    other = kv_flip(send, 1)
    half = jax.ShapeDtypeStruct((keep.shape[0], width // 2 + LANES), BF16)
    keep, send = pl.pallas_call(
        join_kernel,
        in_specs=[SMEM, VMEM, VMEM],
        out_specs=[VMEM, VMEM],
        out_shape=[half, half],
        compiler_params=params(60),
        name="join",
    )(after(chip.reshape(1), arrived[2], arrived[1], blocks[0][1], w1), keep, other)
    other = kv_flip(send, 2)
    blocks[1] = shared(after(arrived[1], keep))
    blocks[2] = shared(after(arrived[2], keep))
    tokens = jax.ShapeDtypeStruct(residual_in.shape, BF16)
    partial, send = pl.pallas_call(
        project_kernel,
        in_specs=[SMEM] + [VMEM] * 4,
        out_specs=[VMEM, VMEM],
        out_shape=[jax.ShapeDtypeStruct(residual_in.shape, F32), tokens],
        scratch_shapes=[
            pltpu.VMEM((keep.shape[0], width // 2), BF16),
            pltpu.VMEM((keep.shape[0], width), F32),
        ],
        compiler_params=params(16),
        name="project",
    )(own, keep, other, out_weight, w1)
    other = kv_flip(send, 2)
    normed, residual = pl.pallas_call(
        norm_kernel,
        in_specs=[VMEM] * 4,
        out_specs=[VMEM, VMEM],
        out_shape=[tokens, tokens],
        compiler_params=params(60),
        name="norm",
    )(partial, other, residual_in, norm_gain.reshape(1, width))

    order = (0, 1, 2, 3)
    deep = width // OUTER

    def laid(indices, base, *others):
        spots, parts = [], []
        for index in indices:
            for mine in (True, False):
                spots.append((index * deep - base, deep // 2, mine))
                parts.append(blocks[index][0 if mine else 1])
        return place(parts, spots, after(y_place, *others))

    near = [laid((0, 1), 0, normed)]
    count = residual_in.shape[0]
    ready = after(normed, arrived[3])
    here = {0: normed, 1: z_flip(ready, 1), 3: z_flip(ready, 3)}
    here[2] = z_flip(after(ready, here[1]), 2)
    there = {s: kv_flip(here[s], 2) for s in order}
    blocks[3] = shared(after(arrived[3], blocks[2][1], normed))
    near.append(laid((2, 3), 2 * deep, there[0], there[1], here[3]))
    weights = near + [kv_flip(part, 1) for part in near]

    def added(a, b):
        return (a.astype(F32) + b.astype(F32)).astype(BF16)

    mlp = residual.astype(F32)
    kept, arrivals, terms = [], [], []
    for s in (3, 1, 2, 0):
        turn = after(z, *kept[-1:], *arrivals[:-1], *terms[:-2])
        keep, send = feed(main, tail, order, turn, [here[s], there[s]], weights)
        other = kv_flip(send, 2)
        kept.append(keep)
        arrivals.append(other)
        term = added(keep, other)
        terms.append(z_flip(term, s) if s else term)
        mlp = mlp + terms[-1].astype(F32)
    return mlp.astype(BF16)


def solution(mesh):
    placed = (
        P(("dp", "kv"), None),
        P("dp", None),
        P("dp", "kv", None),
        P("dp", "kv", None),
        P("dp"),
        P("kv", None),
        P(),
        P("dp", "kv"),
        P("dp", "kv"),
        P("kv", "dp"),
    )
    return jax.shard_map(
        per_device, mesh=mesh, in_specs=placed, out_specs=P(("dp", "kv"), None), check_vma=False
    )
```

```python
import functools

import jax
import jax.numpy as jnp
from jax import lax
from jax.experimental import pallas as pl
from jax.experimental.pallas import tpu as pltpu
from jax.sharding import PartitionSpec as P

H = 24
HD = 64
KVH = 8
LANES = 128
SUM_HIGH = 32
SUM_LOW = 64
OUTER = 4

VMEM = pl.BlockSpec(memory_space=pltpu.VMEM)
SMEM = pl.BlockSpec(memory_space=pltpu.SMEM)
HBM = pl.BlockSpec(memory_space=pl.ANY)
NT = (((1,), (1,)), ((), ()))
BF16 = jnp.bfloat16
F32 = jnp.float32


def params(mib):
    return pltpu.CompilerParams(vmem_limit_bytes=mib * 1024 * 1024)


def iota(shape, dim):
    return lax.broadcasted_iota(jnp.int32, shape, dim)


def dot(a, b):
    return jnp.dot(a, b, preferred_element_type=F32)


def one_hot(condition):
    return jnp.where(condition, 1.0, 0.0).astype(BF16)


def pack_kernel(main, tail, cuts, z_ref, gate_ref, up_ref, down_ref, *refs):
    outs, slots, (weights, sems, in_sems) = refs[: len(cuts)], refs[len(cuts) : -3], refs[-3:]
    tail_at = OUTER * main
    second = 2 * main + LANES
    total = weights.shape[1]
    step = total // 2 if total % 32 == 0 else total
    loads, copies = [], []
    for start in range(0, total, step):
        for index, ref in enumerate((gate_ref, up_ref, down_ref)):
            pick = pl.ds(start, step)
            loads.append(pltpu.make_async_copy(ref.at[pick], weights.at[index, pick], in_sems.at[len(loads)]))
            loads[-1].start()
    shape = (OUTER * tail, LANES)
    lane = iota(shape, 1)
    targets = [z_ref[0] ^ shift for shift in cuts]
    firsts = [one_hot((lane < tail) & (iota(shape, 0) == lane + target * tail)) for target in targets]
    seconds = [
        one_hot((lane >= tail) & (lane < 2 * tail) & (iota(shape, 0) == lane - tail + target * tail))
        for target in targets
    ]
    for start in range(0, total, step):
        for load in loads[start // step * 3 : start // step * 3 + 3]:
            load.wait()
        pick = slice(start, start + step)
        gate, up, down = (weights.at[index] for index in range(3))
        for index, out in enumerate(slots):
            column = pl.multiple_of(targets[index] * main, LANES)
            out[pick, :main] = gate[pick, pl.ds(column, main)]
            out[pick, main : 2 * main] = up[pick, pl.ds(column, main)]
            out[pick, second : second + main] = down[pick, pl.ds(column, main)]
            ends = dot(gate[pick, tail_at:], firsts[index]) + dot(up[pick, tail_at:], seconds[index])
            out[pick, 2 * main : second] = ends.astype(BF16)
            out[pick, second + main :] = dot(down[pick, tail_at:], firsts[index]).astype(BF16)
            rows = pl.ds(start, step)
            copies.append(pltpu.make_async_copy(out.at[rows], outs[index].at[rows], sems.at[len(copies)]))
            copies[-1].start()
    for copy in copies:
        copy.wait()


def place_kernel(spots, at_ref, *refs):
    blocks, out = refs[:-1], refs[-1]
    for block, (start, step, mine) in zip(blocks, spots):
        side = at_ref[0] if mine else 1 - at_ref[0]
        out[pl.ds(pl.multiple_of(start + step * side, 16), block.shape[0]), :] = block[...]


def place(blocks, spots, at):
    rows = sum(block.shape[0] for block in blocks)
    return pl.pallas_call(
        functools.partial(place_kernel, spots),
        in_specs=[SMEM] + [VMEM] * len(blocks),
        out_specs=VMEM,
        out_shape=jax.ShapeDtypeStruct((rows, blocks[0].shape[1]), BF16),
        compiler_params=params(16),
        name="place",
    )(at, *blocks)


def attention_kernel(at_ref, lengths_ref, q_hbm, k_hbm, v_hbm, keep_ref, send_ref, q_ref, k_ref, v_ref, bias, result, stats, lines, sems):
    rows, width = q_ref.shape
    requests, slab, _ = k_ref.shape
    block = 2 * (H // KVH) * HD
    steps = width // block
    span = rows - (requests - 1)
    heads = block // HD
    group = H // KVH
    first_key, half_row = at_ref[0] * slab, lax.rem(at_ref[0], 2)

    def load(source, target, index):
        return pltpu.make_async_copy(source, target, sems.at[index])

    loads = [load(q_hbm, q_ref, 0)]
    loads += [load(k_hbm.at[r], k_ref.at[r], 1 + r) for r in range(requests)]
    loads += [load(v_hbm.at[r], v_ref.at[r], 1 + requests + r) for r in range(requests)]
    order = [0, 1, 1 + requests] + [i for i in range(2, len(loads)) if i != 1 + requests]
    for index in order:
        loads[index].start()

    place = first_key + iota((slab, rows), 0)
    limit = lengths_ref[0] - span + iota((slab, rows), 1)
    bias[...] = jnp.where(place <= limit, 0.0, -1e30)
    stats[...] = jnp.zeros_like(stats)
    lines[...] = jnp.zeros_like(lines)

    lane = iota((1, LANES), 1)
    low_lanes = lane < HD

    def in_half(a):
        return low_lanes if a == 0 else ~low_lanes

    def placed(value, h):
        return pltpu.roll(value, HD, 1) if h % 2 != h // group else value

    def record(old, column, top, total):
        high = total.astype(BF16).astype(F32)
        old = jnp.where(lane == column, top, old)
        old = jnp.where(lane == column + SUM_HIGH, high, old)
        return jnp.where(lane == column + SUM_LOW, total - high, old)

    for index in order[:3]:
        loads[index].wait()

    def one(step):
        near = pl.ds(step * LANES, LANES)

        def aligned(h):
            column = step * block + h // 2 * LANES
            tile = placed(q_ref[:, pl.ds(column, LANES)].astype(F32) * HD**-0.5, h)
            return jnp.where(in_half(h // group), tile, 0.0)

        keys, value = k_ref[0, :, near], v_ref[0, :, near]
        stat = stats[...]
        queries = [aligned(h) for h in range(heads)]
        sub = iota((8, 1), 0)
        for r in range(1, requests):
            line = jnp.zeros((8, LANES), F32)
            for h in range(heads):
                last = queries[h][rows - 8 :][8 - requests + r : 9 - requests + r]
                line = jnp.where(sub == h, jnp.broadcast_to(last, (8, LANES)), line)
            lines[r - 1, pl.ds(step * 8, 8), near] = line
        outs = []
        for a in range(2):
            query = jnp.concatenate(queries[a * group : (a + 1) * group], 0).astype(BF16)
            scores = lax.dot_general(keys, query, NT, preferred_element_type=F32)
            scores = scores + jnp.concatenate([bias[...]] * group, 1)
            top = jnp.maximum(jnp.max(scores, axis=0, keepdims=True), -1e29).astype(BF16).astype(F32)
            weights = jnp.exp((scores - top).astype(BF16))
            values = jnp.where(in_half(a), value, jnp.ones((), BF16)).astype(F32).T.astype(BF16)
            out = dot(values, weights).T
            top = jnp.broadcast_to(top, (8, top.shape[1])).T[:, :1]
            total = jnp.where(in_half(a), pltpu.roll(out, HD, 1), out)
            for r in range(group):
                h = a * group + r
                pick = slice(r * rows, (r + 1) * rows)
                stat = record(stat, step * heads + h, top[pick], total[pick])
                outs.append(placed(out[pick], h))
                if h % 2 == 1:
                    column = step * block + h // 2 * LANES
                    result[:, pl.ds(column, LANES)] = jnp.where(low_lanes, outs[h - 1], outs[h])
        stats[...] = stat

    for step in range(steps):
        one(step)
    count = 8 * steps
    sub, column = iota((count, 1), 0), iota((1, LANES), 1)
    spot = sub // 8 * heads + sub % 8
    live = sub % 8 < heads
    for r in range(1, requests):
        loads[1 + r].wait()
        loads[1 + requests + r].wait()
        row = rows - requests + r
        scores = lax.dot_general(lines[r - 1].astype(BF16), k_ref[r], NT, preferred_element_type=F32)
        usable = first_key + iota((1, slab), 1) < lengths_ref[r]
        scores = jnp.where(usable, scores, -1e30)
        top = jnp.maximum(jnp.max(scores, axis=1, keepdims=True), -1e29).astype(BF16).astype(F32)
        weights = jnp.exp(scores - top)
        total = jnp.sum(weights, axis=1, keepdims=True)
        out = dot(weights.astype(BF16), v_ref[r])
        high = total.astype(BF16).astype(F32)
        stat = jnp.where(live & (column == spot), top, 0.0)
        stat = stat + jnp.where(live & (column == spot + SUM_HIGH), high, 0.0)
        stat = stat + jnp.where(live & (column == spot + SUM_LOW), total - high, 0.0)
        stats[row : row + 1, :] = jnp.sum(stat, axis=0, keepdims=True)
        for step in range(steps):
            tile = out[8 * step : 8 * step + 8, step * LANES : (step + 1) * LANES]
            turned = pltpu.roll(tile, HD, 1)
            for h in range(0, heads, 2):
                low = (turned if h // group else tile)[h : h + 1]
                high = (tile if (h + 1) // group else turned)[h + 1 : h + 2]
                at = step * block + h // 2 * LANES
                result[row : row + 1, at : at + LANES] = jnp.where(low_lanes, low, high)

    quarter = rows // 4
    for ref, which in ((keep_ref, half_row), (send_ref, 1 - half_row)):
        for part in range(2):
            pick = pl.ds(pl.multiple_of((2 * part + which) * quarter, 16), quarter)
            ref[part * quarter : (part + 1) * quarter, :width] = result[pick, :].astype(BF16)
            ref[part * quarter : (part + 1) * quarter, width:] = stats[pick, :].astype(BF16)


def attention(queries, keys, values, at, lengths):
    rows, width = queries.shape
    requests, slab, depth = keys.shape
    half = jax.ShapeDtypeStruct((rows // 2, width + LANES), BF16)
    return pl.pallas_call(
        attention_kernel,
        in_specs=[SMEM, SMEM, HBM, HBM, HBM],
        out_specs=[VMEM, VMEM],
        out_shape=[half, half],
        scratch_shapes=[
            pltpu.VMEM(queries.shape, BF16),
            pltpu.VMEM(keys.shape, BF16),
            pltpu.VMEM(values.shape, BF16),
            pltpu.VMEM((slab, rows), F32),
            pltpu.VMEM((rows, width), F32),
            pltpu.VMEM((rows, LANES), F32),
            pltpu.VMEM((requests - 1, 8 * width // (2 * (H // KVH) * HD), depth), F32),
            pltpu.SemaphoreType.DMA((1 + 2 * requests,)),
        ],
        compiler_params=params(56),
        name="attention",
    )(at, lengths, queries, keys, values)


def expanded(scale, width):
    high = scale.astype(BF16).astype(F32)
    both = (high + pltpu.roll(scale - high, SUM_HIGH, 1)).astype(BF16)
    shape = (LANES, width)
    k, column = iota(shape, 0), iota(shape, 1)
    spread = one_hot(((k & (SUM_HIGH - 1)) == column // HD) & (k < 2 * SUM_HIGH))
    return dot(both, spread)


def merged(parts, width):
    tiles = [part[:, width:].astype(F32) for part in parts]
    valid = iota((1, LANES), 1) < width // HD
    top = functools.reduce(jnp.maximum, tiles)
    scales = [jnp.where(valid, jnp.exp(tile - top), 0.0) for tile in tiles]
    sums = [pltpu.roll(tile, LANES - SUM_HIGH, 1) + pltpu.roll(tile, LANES - SUM_LOW, 1) for tile in tiles]
    total = functools.reduce(jnp.add, [a * b for a, b in zip(sums, scales)])
    return top, total, scales, valid


def weighted(parts, scales, width):
    terms = [part[:, :width].astype(F32) * expanded(scale, width) for part, scale in zip(parts, scales)]
    return functools.reduce(jnp.add, terms).astype(BF16)


def join_kernel(at_ref, own_ref, other_ref, keep_ref, send_ref):
    width, part_width = own_ref.shape[1] - LANES, keep_ref.shape[1] - LANES
    own, other = own_ref[...], other_ref[...]
    top, total, scales, _ = merged([own, other], width)
    valid = iota((1, LANES), 1) < part_width // HD
    for ref, which in ((send_ref, 1 - at_ref[0]), (keep_ref, at_ref[0])):

        def here(tile):
            moved = pltpu.roll(tile, LANES - part_width // HD, 1)
            return jnp.where(valid, jnp.where(which == 1, moved, tile), 0.0)

        pick = pl.ds(pl.multiple_of(which * part_width, LANES), part_width)
        ref[:, :part_width] = weighted([own_ref[:, pick], other_ref[:, pick]], [here(scale) for scale in scales], part_width)
        sums = here(total)
        high = sums.astype(BF16).astype(F32)
        stat = here(top) + pltpu.roll(high, SUM_HIGH, 1) + pltpu.roll(sums - high, SUM_LOW, 1)
        ref[:, part_width:] = stat.astype(BF16)


def project_kernel(at_ref, own_ref, other_ref, w0, w1, keep_ref, send_ref, attended, mixed):
    width = own_ref.shape[1] - LANES
    parts = [own_ref[...], other_ref[...]]
    _, total, scales, valid = merged(parts, width)
    inverse = 1.0 / jnp.where(valid, total, 1.0)
    attended[...] = weighted(parts, [scale * inverse for scale in scales], width)
    depth = w0.shape[0]
    core, chip = lax.rem(at_ref[0], 2), at_ref[0] // 2
    first = dot(attended[:, pl.ds(pl.multiple_of(core * depth, LANES), depth)], w0[...])
    second = dot(attended[:, pl.ds(pl.multiple_of((1 - core) * depth, LANES), depth)], w1[...])
    mixed[...] = first + second
    rows = keep_ref.shape[0]
    keep_ref[...] = mixed[pl.ds(pl.multiple_of(chip * rows, 16), rows), :]
    send_ref[...] = mixed[pl.ds(pl.multiple_of((1 - chip) * rows, 16), rows), :].astype(BF16)


def norm_kernel(keep_ref, other_ref, residual_ref, gain_ref, normed_ref, out_ref):
    mixed = keep_ref[...] + other_ref[...].astype(F32)
    residual = (residual_ref[...].astype(F32) + mixed).astype(BF16)
    out_ref[...] = residual
    wide = residual.astype(F32)
    scale = lax.rsqrt(jnp.mean(wide * wide, axis=-1, keepdims=True) + 1e-05)
    normed_ref[...] = (wide * scale * gain_ref[...]).astype(BF16)


def feed_kernel(main, tail, count, order, z_ref, *refs):
    tokens, weights = refs[:count], refs[count : count + 4]
    keep_ref, send_ref, x = refs[count + 4 :]
    width = x.shape[1]
    block = width // OUTER
    rows = tokens[0].shape[0]
    columns = [pl.multiple_of((z_ref[0] ^ b) * block, LANES) for b in order]
    for index, ref in enumerate(tokens):
        for b in range(OUTER):
            x[index * rows : (index + 1) * rows, b * block : (b + 1) * block] = ref[:, pl.ds(columns[b], block)]

    def silu(v):
        return v / (1.0 + jnp.exp(-v))

    lane = iota((1, LANES), 1)
    second = 2 * main + LANES
    depth = weights[0].shape[0]
    hidden = []
    for first, last in (weights[:2], weights[2:]):
        sums = dot(x[:, :depth], first[:, :second]) + dot(x[:, depth:], last[:, :second])
        end = sums[:, 2 * main :]
        ends = silu(end) * pltpu.roll(end, LANES - tail, 1)
        hidden.append(
            jnp.concatenate(
                [
                    (silu(sums[:, :main]) * sums[:, main : 2 * main]).astype(BF16),
                    jnp.where(lane < tail, ends, 0.0).astype(BF16),
                ],
                1,
            )
        )
    half = count * rows // 2
    for b in range(OUTER):
        place = b * block
        which = place // depth
        pick = slice(place - which * depth, place - which * depth + block)
        out = lax.dot_general(hidden[0], weights[which][pick, second:], NT, preferred_element_type=F32)
        out = out + lax.dot_general(hidden[1], weights[2 + which][pick, second:], NT, preferred_element_type=F32)
        out = out.astype(BF16)
        keep_ref[:, pl.ds(columns[b], block)] = out[:half]
        send_ref[:, pl.ds(columns[b], block)] = out[half:]


def feed(main, tail, order, z, tokens, weights):
    rows, width = tokens[0].shape
    count = len(tokens)
    half = jax.ShapeDtypeStruct((count * rows // 2, width), BF16)
    return pl.pallas_call(
        functools.partial(feed_kernel, main, tail, count, order),
        in_specs=[SMEM] + [VMEM] * (count + 4),
        out_specs=[VMEM] * 2,
        out_shape=[half, half],
        scratch_shapes=[pltpu.VMEM((count * rows, width), BF16)],
        compiler_params=params(24),
        name="feed",
    )(z, *tokens, *weights)


def after(value, *others):
    return lax.optimization_barrier((value, *others))[0]


def per_device(
    residual_in,
    queries,
    key_cache,
    value_cache,
    cache_lengths,
    out_weight,
    norm_gain,
    gate_weight,
    up_weight,
    down_weight,
):
    dp_size, kv_size = lax.axis_size("dp"), lax.axis_size("kv")
    inner = dp_size // OUTER
    dp_index, kv_index = lax.axis_index("dp"), lax.axis_index("kv")
    z, y = (dp_index // inner).reshape(1), dp_index % inner
    chip = kv_index // 2
    units = gate_weight.shape[1]
    main = units // OUTER // LANES * LANES
    tail = units // OUTER - main
    width = residual_in.shape[1]

    def kv_flip(a, bit):
        return lax.ppermute(a, "kv", [(i, i ^ bit) for i in range(kv_size)])

    def z_flip(a, by):
        return lax.ppermute(a, "dp", [(i, i ^ (by * inner)) for i in range(dp_size)])

    def y_flip(a, bit):
        return lax.ppermute(a, "dp", [(i, i ^ bit) for i in range(dp_size)])

    rows = gate_weight.shape[0]
    cuts = list(range(OUTER))
    sizes = [(rows, 3 * main + 2 * LANES)] * OUTER
    packed = pl.pallas_call(
        functools.partial(pack_kernel, main, tail, cuts),
        in_specs=[SMEM] + [HBM] * 3,
        out_specs=[HBM] * len(cuts),
        out_shape=[jax.ShapeDtypeStruct(size, BF16) for size in sizes],
        scratch_shapes=[pltpu.VMEM(size, BF16) for size in sizes]
        + [
            pltpu.VMEM((3,) + gate_weight.shape, BF16),
            pltpu.SemaphoreType.DMA((2 * OUTER,)),
            pltpu.SemaphoreType.DMA((6,)),
        ],
        compiler_params=params(60),
        name="pack",
    )(z, gate_weight, up_weight, down_weight.T)

    def shared(block):
        bit = 1
        while 2 * bit < inner:
            other = y_flip(block, bit)
            upper = (y & bit) > 0
            block = jnp.concatenate([jnp.where(upper, other, block), jnp.where(upper, block, other)], 0)
            bit *= 2
        return [block, y_flip(block, bit)]

    y_place = (y >= inner // 2).astype(jnp.int32).reshape(1)

    arrived = {index: z_flip(packed[index], index) for index in (2, 1)}
    blocks = {0: shared(packed[0])}
    w1 = kv_flip(after(out_weight, packed[0]), 1)
    own = kv_index.reshape(1)
    keep, send = attention(queries, key_cache, value_cache, after(own, *packed), cache_lengths)
    arrived[3] = z_flip(after(packed[3], arrived[2]), 3)
    other = kv_flip(send, 1)
    half = jax.ShapeDtypeStruct((keep.shape[0], width // 2 + LANES), BF16)
    keep, send = pl.pallas_call(
        join_kernel,
        in_specs=[SMEM, VMEM, VMEM],
        out_specs=[VMEM, VMEM],
        out_shape=[half, half],
        compiler_params=params(60),
        name="join",
    )(after(chip.reshape(1), arrived[2], arrived[1], blocks[0][1], w1), keep, other)
    other = kv_flip(send, 2)
    blocks[1] = shared(after(arrived[1], keep))
    blocks[2] = shared(after(arrived[2], keep))
    tokens = jax.ShapeDtypeStruct(residual_in.shape, BF16)
    partial, send = pl.pallas_call(
        project_kernel,
        in_specs=[SMEM] + [VMEM] * 4,
        out_specs=[VMEM, VMEM],
        out_shape=[jax.ShapeDtypeStruct(residual_in.shape, F32), tokens],
        scratch_shapes=[
            pltpu.VMEM((keep.shape[0], width // 2), BF16),
            pltpu.VMEM((keep.shape[0], width), F32),
        ],
        compiler_params=params(16),
        name="project",
    )(own, keep, other, out_weight, w1)
    other = kv_flip(send, 2)
    normed, residual = pl.pallas_call(
        norm_kernel,
        in_specs=[VMEM] * 4,
        out_specs=[VMEM, VMEM],
        out_shape=[tokens, tokens],
        compiler_params=params(60),
        name="norm",
    )(partial, other, residual_in, norm_gain.reshape(1, width))

    order = (0, 1, 2, 3)
    deep = width // OUTER

    def laid(indices, base, *others):
        spots, parts = [], []
        for index in indices:
            for mine in (True, False):
                spots.append((index * deep - base, deep // 2, mine))
                parts.append(blocks[index][0 if mine else 1])
        return place(parts, spots, after(y_place, *others))

    near = [laid((0, 1), 0, normed)]
    count = residual_in.shape[0]
    ready = after(normed, arrived[3])
    here = {0: normed, 1: z_flip(ready, 1), 3: z_flip(ready, 3)}
    here[2] = z_flip(ready, 2)
    there = {s: kv_flip(here[s], 2) for s in order}
    blocks[3] = shared(after(arrived[3], blocks[2][1], normed))
    near.append(laid((2, 3), 2 * deep, there[0], there[1], here[3]))
    weights = near + [kv_flip(part, 1) for part in near]

    def added(a, b):
        return (a.astype(F32) + b.astype(F32)).astype(BF16)

    mlp = residual.astype(F32)
    kept, arrivals, terms = [], [], []
    for s in (3, 1, 2, 0):
        turn = after(z, *kept[-1:], *arrivals[:-1], *terms[:-2])
        keep, send = feed(main, tail, order, turn, [here[s], there[s]], weights)
        other = kv_flip(send, 2)
        kept.append(keep)
        arrivals.append(other)
        term = added(keep, other)
        terms.append(z_flip(term, s) if s else term)
        mlp = mlp + terms[-1].astype(F32)
    return mlp.astype(BF16)


def solution(mesh):
    placed = (
        P(("dp", "kv"), None),
        P("dp", None),
        P("dp", "kv", None),
        P("dp", "kv", None),
        P("dp"),
        P("kv", None),
        P(),
        P("dp", "kv"),
        P("dp", "kv"),
        P("kv", "dp"),
    )
    return jax.shard_map(
        per_device, mesh=mesh, in_specs=placed, out_specs=P(("dp", "kv"), None), check_vma=False
    )
```

```python
import functools

import jax
import jax.numpy as jnp
from jax import lax
from jax.experimental import pallas as pl
from jax.experimental.pallas import tpu as pltpu
from jax.sharding import PartitionSpec as P

H = 24
HD = 64
KVH = 8
LANES = 128
SUM_HIGH = 32
SUM_LOW = 64
TOP_LOW = 96
OUTER = 4

VMEM = pl.BlockSpec(memory_space=pltpu.VMEM)
SMEM = pl.BlockSpec(memory_space=pltpu.SMEM)
HBM = pl.BlockSpec(memory_space=pl.ANY)
NT = (((1,), (1,)), ((), ()))
BF16 = jnp.bfloat16
F32 = jnp.float32


def params(mib):
    return pltpu.CompilerParams(vmem_limit_bytes=mib * 1024 * 1024)


def iota(shape, dim):
    return lax.broadcasted_iota(jnp.int32, shape, dim)


def dot(a, b):
    return jnp.dot(a, b, preferred_element_type=F32)


def rounded(value):
    return value.astype(BF16).astype(F32)


def two_part(value):
    high = rounded(value)
    return high + rounded(value - high)


def one_hot(condition):
    return jnp.where(condition, 1.0, 0.0).astype(BF16)


def pack_kernel(main, tail, cuts, z_ref, gate_ref, up_ref, down_ref, *refs):
    outs, slots, (weights, sems, in_sems) = refs[: len(cuts)], refs[len(cuts) : -3], refs[-3:]
    tail_at = OUTER * main
    second = 2 * main + LANES
    total = weights.shape[1]
    step = total // 2 if total % 32 == 0 else total
    loads, copies = [], []
    for start in range(0, total, step):
        for index, ref in enumerate((gate_ref, up_ref, down_ref)):
            pick = pl.ds(start, step)
            loads.append(pltpu.make_async_copy(ref.at[pick], weights.at[index, pick], in_sems.at[len(loads)]))
            loads[-1].start()
    shape = (OUTER * tail, LANES)
    lane = iota(shape, 1)
    targets = [z_ref[0] ^ shift for shift in cuts]
    firsts = [one_hot((lane < tail) & (iota(shape, 0) == lane + target * tail)) for target in targets]
    seconds = [
        one_hot((lane >= tail) & (lane < 2 * tail) & (iota(shape, 0) == lane - tail + target * tail))
        for target in targets
    ]
    for start in range(0, total, step):
        for load in loads[start // step * 3 : start // step * 3 + 3]:
            load.wait()
        pick = slice(start, start + step)
        gate, up, down = (weights.at[index] for index in range(3))
        for index, out in enumerate(slots):
            column = pl.multiple_of(targets[index] * main, LANES)
            out[pick, :main] = gate[pick, pl.ds(column, main)]
            out[pick, main : 2 * main] = up[pick, pl.ds(column, main)]
            out[pick, second : second + main] = down[pick, pl.ds(column, main)]
            ends = dot(gate[pick, tail_at:], firsts[index]) + dot(up[pick, tail_at:], seconds[index])
            out[pick, 2 * main : second] = ends.astype(BF16)
            out[pick, second + main :] = dot(down[pick, tail_at:], firsts[index]).astype(BF16)
            rows = pl.ds(start, step)
            copies.append(pltpu.make_async_copy(out.at[rows], outs[index].at[rows], sems.at[len(copies)]))
            copies[-1].start()
    for copy in copies:
        copy.wait()


def place_kernel(spots, at_ref, *refs):
    blocks, out = refs[:-1], refs[-1]
    for block, (start, step, mine) in zip(blocks, spots):
        side = at_ref[0] if mine else 1 - at_ref[0]
        out[pl.ds(pl.multiple_of(start + step * side, 16), block.shape[0]), :] = block[...]


def place(blocks, spots, at):
    rows = sum(block.shape[0] for block in blocks)
    return pl.pallas_call(
        functools.partial(place_kernel, spots),
        in_specs=[SMEM] + [VMEM] * len(blocks),
        out_specs=VMEM,
        out_shape=jax.ShapeDtypeStruct((rows, blocks[0].shape[1]), BF16),
        compiler_params=params(16),
        name="place",
    )(at, *blocks)


def attention_kernel(at_ref, lengths_ref, q_hbm, k_hbm, v_hbm, keep_ref, send_ref, q_ref, k_ref, v_ref, bias, result, stats, lines, sems):
    rows, width = q_ref.shape
    requests, slab, _ = k_ref.shape
    block = 2 * (H // KVH) * HD
    steps = width // block
    span = rows - (requests - 1)
    heads = block // HD
    group = H // KVH
    first_key, half_row = at_ref[0] * slab, lax.rem(at_ref[0], 2)

    def load(source, target, index):
        return pltpu.make_async_copy(source, target, sems.at[index])

    loads = [load(q_hbm, q_ref, 0)]
    loads += [load(k_hbm.at[r], k_ref.at[r], 1 + r) for r in range(requests)]
    loads += [load(v_hbm.at[r], v_ref.at[r], 1 + requests + r) for r in range(requests)]
    order = [0, 1, 1 + requests] + [i for i in range(2, len(loads)) if i != 1 + requests]
    for index in order:
        loads[index].start()

    place = first_key + iota((slab, rows), 0)
    limit = lengths_ref[0] - span + iota((slab, rows), 1)
    bias[...] = jnp.where(place <= limit, 0.0, -1e30)
    stats[...] = jnp.zeros_like(stats)
    lines[...] = jnp.zeros_like(lines)

    lane = iota((1, LANES), 1)
    low_lanes = lane < HD

    def in_half(a):
        return low_lanes if a == 0 else ~low_lanes

    def placed(value, h):
        return pltpu.roll(value, HD, 1) if h % 2 != h // group else value

    def record(old, column, top, total):
        high = total.astype(BF16).astype(F32)
        top_high = rounded(top)
        old = jnp.where(lane == column, top_high, old)
        old = jnp.where(lane == column + TOP_LOW, top - top_high, old)
        old = jnp.where(lane == column + SUM_HIGH, high, old)
        return jnp.where(lane == column + SUM_LOW, total - high, old)

    for index in order[:3]:
        loads[index].wait()

    def one(step):
        near = pl.ds(step * LANES, LANES)

        def aligned(h):
            column = step * block + h // 2 * LANES
            tile = placed(q_ref[:, pl.ds(column, LANES)].astype(F32) * HD**-0.5, h)
            return jnp.where(in_half(h // group), tile, 0.0)

        keys, value = k_ref[0, :, near], v_ref[0, :, near]
        stat = stats[...]
        queries = [aligned(h) for h in range(heads)]
        sub = iota((8, 1), 0)
        for r in range(1, requests):
            line = jnp.zeros((8, LANES), F32)
            for h in range(heads):
                last = queries[h][rows - 8 :][8 - requests + r : 9 - requests + r]
                line = jnp.where(sub == h, jnp.broadcast_to(last, (8, LANES)), line)
            lines[r - 1, pl.ds(step * 8, 8), near] = line
        outs = []
        for a in range(2):
            query = jnp.concatenate(queries[a * group : (a + 1) * group], 0).astype(BF16)
            scores = lax.dot_general(keys, query, NT, preferred_element_type=F32)
            scores = scores + jnp.concatenate([bias[...]] * group, 1)
            top = two_part(jnp.maximum(jnp.max(scores, axis=0, keepdims=True), -1e29))
            weights = jnp.exp((scores - top).astype(BF16))
            values = jnp.where(in_half(a), value, jnp.ones((), BF16)).astype(F32).T.astype(BF16)
            out = dot(values, weights).T
            top = jnp.broadcast_to(top, (8, top.shape[1])).T[:, :1]
            total = jnp.where(in_half(a), pltpu.roll(out, HD, 1), out)
            for r in range(group):
                h = a * group + r
                pick = slice(r * rows, (r + 1) * rows)
                stat = record(stat, step * heads + h, top[pick], total[pick])
                outs.append(placed(out[pick], h))
                if h % 2 == 1:
                    column = step * block + h // 2 * LANES
                    result[:, pl.ds(column, LANES)] = jnp.where(low_lanes, outs[h - 1], outs[h])
        stats[...] = stat

    for step in range(steps):
        one(step)
    count = 8 * steps
    sub, column = iota((count, 1), 0), iota((1, LANES), 1)
    spot = sub // 8 * heads + sub % 8
    live = sub % 8 < heads
    for r in range(1, requests):
        loads[1 + r].wait()
        loads[1 + requests + r].wait()
        row = rows - requests + r
        scores = lax.dot_general(lines[r - 1].astype(BF16), k_ref[r], NT, preferred_element_type=F32)
        usable = first_key + iota((1, slab), 1) < lengths_ref[r]
        scores = jnp.where(usable, scores, -1e30)
        top = two_part(jnp.maximum(jnp.max(scores, axis=1, keepdims=True), -1e29))
        weights = jnp.exp(scores - top)
        total = jnp.sum(weights, axis=1, keepdims=True)
        out = dot(weights.astype(BF16), v_ref[r])
        high = total.astype(BF16).astype(F32)
        top_high = rounded(top)
        stat = jnp.where(live & (column == spot), top_high, 0.0)
        stat = stat + jnp.where(live & (column == spot + TOP_LOW), top - top_high, 0.0)
        stat = stat + jnp.where(live & (column == spot + SUM_HIGH), high, 0.0)
        stat = stat + jnp.where(live & (column == spot + SUM_LOW), total - high, 0.0)
        stats[row : row + 1, :] = jnp.sum(stat, axis=0, keepdims=True)
        for step in range(steps):
            tile = out[8 * step : 8 * step + 8, step * LANES : (step + 1) * LANES]
            turned = pltpu.roll(tile, HD, 1)
            for h in range(0, heads, 2):
                low = (turned if h // group else tile)[h : h + 1]
                high = (tile if (h + 1) // group else turned)[h + 1 : h + 2]
                at = step * block + h // 2 * LANES
                result[row : row + 1, at : at + LANES] = jnp.where(low_lanes, low, high)

    quarter = rows // 4
    for ref, which in ((keep_ref, half_row), (send_ref, 1 - half_row)):
        for part in range(2):
            pick = pl.ds(pl.multiple_of((2 * part + which) * quarter, 16), quarter)
            ref[part * quarter : (part + 1) * quarter, :width] = result[pick, :].astype(BF16)
            ref[part * quarter : (part + 1) * quarter, width:] = stats[pick, :].astype(BF16)


def attention(queries, keys, values, at, lengths):
    rows, width = queries.shape
    requests, slab, depth = keys.shape
    half = jax.ShapeDtypeStruct((rows // 2, width + LANES), BF16)
    return pl.pallas_call(
        attention_kernel,
        in_specs=[SMEM, SMEM, HBM, HBM, HBM],
        out_specs=[VMEM, VMEM],
        out_shape=[half, half],
        scratch_shapes=[
            pltpu.VMEM(queries.shape, BF16),
            pltpu.VMEM(keys.shape, BF16),
            pltpu.VMEM(values.shape, BF16),
            pltpu.VMEM((slab, rows), F32),
            pltpu.VMEM((rows, width), F32),
            pltpu.VMEM((rows, LANES), F32),
            pltpu.VMEM((requests - 1, 8 * width // (2 * (H // KVH) * HD), depth), F32),
            pltpu.SemaphoreType.DMA((1 + 2 * requests,)),
        ],
        compiler_params=params(56),
        name="attention",
    )(at, lengths, queries, keys, values)


def expanded(scale, width):
    high = scale.astype(BF16).astype(F32)
    both = (high + pltpu.roll(scale - high, SUM_HIGH, 1)).astype(BF16)
    shape = (LANES, width)
    k, column = iota(shape, 0), iota(shape, 1)
    spread = one_hot(((k & (SUM_HIGH - 1)) == column // HD) & (k < 2 * SUM_HIGH))
    return dot(both, spread)


def merged(parts, width):
    tiles = [part[:, width:].astype(F32) for part in parts]
    valid = iota((1, LANES), 1) < width // HD
    tops = [tile + pltpu.roll(tile, LANES - TOP_LOW, 1) for tile in tiles]
    top = functools.reduce(jnp.maximum, tops)
    scales = [jnp.where(valid, jnp.exp(one - top), 0.0) for one in tops]
    sums = [pltpu.roll(tile, LANES - SUM_HIGH, 1) + pltpu.roll(tile, LANES - SUM_LOW, 1) for tile in tiles]
    total = functools.reduce(jnp.add, [a * b for a, b in zip(sums, scales)])
    return top, total, scales, valid


def weighted(parts, scales, width):
    terms = [part[:, :width].astype(F32) * expanded(scale, width) for part, scale in zip(parts, scales)]
    return functools.reduce(jnp.add, terms).astype(BF16)


def join_kernel(at_ref, own_ref, other_ref, keep_ref, send_ref):
    width, part_width = own_ref.shape[1] - LANES, keep_ref.shape[1] - LANES
    own, other = own_ref[...], other_ref[...]
    top, total, scales, _ = merged([own, other], width)
    valid = iota((1, LANES), 1) < part_width // HD
    for ref, which in ((send_ref, 1 - at_ref[0]), (keep_ref, at_ref[0])):

        def here(tile):
            moved = pltpu.roll(tile, LANES - part_width // HD, 1)
            return jnp.where(valid, jnp.where(which == 1, moved, tile), 0.0)

        pick = pl.ds(pl.multiple_of(which * part_width, LANES), part_width)
        ref[:, :part_width] = weighted([own_ref[:, pick], other_ref[:, pick]], [here(scale) for scale in scales], part_width)
        sums = here(total)
        high = sums.astype(BF16).astype(F32)
        own_top = here(top)
        top_high = rounded(own_top)
        stat = top_high + pltpu.roll(own_top - top_high, TOP_LOW, 1)
        stat = stat + pltpu.roll(high, SUM_HIGH, 1) + pltpu.roll(sums - high, SUM_LOW, 1)
        ref[:, part_width:] = stat.astype(BF16)


def project_kernel(at_ref, own_ref, other_ref, w0, w1, keep_ref, send_ref, attended, mixed):
    width = own_ref.shape[1] - LANES
    parts = [own_ref[...], other_ref[...]]
    _, total, scales, valid = merged(parts, width)
    inverse = 1.0 / jnp.where(valid, total, 1.0)
    attended[...] = weighted(parts, [scale * inverse for scale in scales], width)
    depth = w0.shape[0]
    core, chip = lax.rem(at_ref[0], 2), at_ref[0] // 2
    first = dot(attended[:, pl.ds(pl.multiple_of(core * depth, LANES), depth)], w0[...])
    second = dot(attended[:, pl.ds(pl.multiple_of((1 - core) * depth, LANES), depth)], w1[...])
    mixed[...] = first + second
    rows = keep_ref.shape[0]
    keep_ref[...] = mixed[pl.ds(pl.multiple_of(chip * rows, 16), rows), :]
    send_ref[...] = mixed[pl.ds(pl.multiple_of((1 - chip) * rows, 16), rows), :].astype(BF16)


def norm_kernel(keep_ref, other_ref, residual_ref, gain_ref, normed_ref, out_ref):
    mixed = keep_ref[...] + other_ref[...].astype(F32)
    residual = (residual_ref[...].astype(F32) + mixed).astype(BF16)
    out_ref[...] = residual
    wide = residual.astype(F32)
    scale = lax.rsqrt(jnp.mean(wide * wide, axis=-1, keepdims=True) + 1e-05)
    normed_ref[...] = (wide * scale * gain_ref[...]).astype(BF16)


def feed_kernel(main, tail, count, order, z_ref, *refs):
    tokens, weights = refs[:count], refs[count : count + 4]
    keep_ref, send_ref, x = refs[count + 4 :]
    width = x.shape[1]
    block = width // OUTER
    rows = tokens[0].shape[0]
    columns = [pl.multiple_of((z_ref[0] ^ b) * block, LANES) for b in order]
    for index, ref in enumerate(tokens):
        for b in range(OUTER):
            x[index * rows : (index + 1) * rows, b * block : (b + 1) * block] = ref[:, pl.ds(columns[b], block)]

    def silu(v):
        return v / (1.0 + jnp.exp(-v))

    lane = iota((1, LANES), 1)
    second = 2 * main + LANES
    depth = weights[0].shape[0]
    hidden = []
    for first, last in (weights[:2], weights[2:]):
        sums = dot(x[:, :depth], first[:, :second]) + dot(x[:, depth:], last[:, :second])
        end = sums[:, 2 * main :]
        ends = silu(end) * pltpu.roll(end, LANES - tail, 1)
        hidden.append(
            jnp.concatenate(
                [
                    (silu(sums[:, :main]) * sums[:, main : 2 * main]).astype(BF16),
                    jnp.where(lane < tail, ends, 0.0).astype(BF16),
                ],
                1,
            )
        )
    half = count * rows // 2
    for b in range(OUTER):
        place = b * block
        which = place // depth
        pick = slice(place - which * depth, place - which * depth + block)
        out = lax.dot_general(hidden[0], weights[which][pick, second:], NT, preferred_element_type=F32)
        out = out + lax.dot_general(hidden[1], weights[2 + which][pick, second:], NT, preferred_element_type=F32)
        out = out.astype(BF16)
        keep_ref[:, pl.ds(columns[b], block)] = out[:half]
        send_ref[:, pl.ds(columns[b], block)] = out[half:]


def feed(main, tail, order, z, tokens, weights):
    rows, width = tokens[0].shape
    count = len(tokens)
    half = jax.ShapeDtypeStruct((count * rows // 2, width), BF16)
    return pl.pallas_call(
        functools.partial(feed_kernel, main, tail, count, order),
        in_specs=[SMEM] + [VMEM] * (count + 4),
        out_specs=[VMEM] * 2,
        out_shape=[half, half],
        scratch_shapes=[pltpu.VMEM((count * rows, width), BF16)],
        compiler_params=params(24),
        name="feed",
    )(z, *tokens, *weights)


def after(value, *others):
    return lax.optimization_barrier((value, *others))[0]


def per_device(
    residual_in,
    queries,
    key_cache,
    value_cache,
    cache_lengths,
    out_weight,
    norm_gain,
    gate_weight,
    up_weight,
    down_weight,
):
    dp_size, kv_size = lax.axis_size("dp"), lax.axis_size("kv")
    inner = dp_size // OUTER
    dp_index, kv_index = lax.axis_index("dp"), lax.axis_index("kv")
    z, y = (dp_index // inner).reshape(1), dp_index % inner
    chip = kv_index // 2
    units = gate_weight.shape[1]
    main = units // OUTER // LANES * LANES
    tail = units // OUTER - main
    width = residual_in.shape[1]

    def kv_flip(a, bit):
        return lax.ppermute(a, "kv", [(i, i ^ bit) for i in range(kv_size)])

    def z_flip(a, by):
        return lax.ppermute(a, "dp", [(i, i ^ (by * inner)) for i in range(dp_size)])

    def y_flip(a, bit):
        return lax.ppermute(a, "dp", [(i, i ^ bit) for i in range(dp_size)])

    rows = gate_weight.shape[0]
    cuts = list(range(OUTER))
    sizes = [(rows, 3 * main + 2 * LANES)] * OUTER
    packed = pl.pallas_call(
        functools.partial(pack_kernel, main, tail, cuts),
        in_specs=[SMEM] + [HBM] * 3,
        out_specs=[HBM] * len(cuts),
        out_shape=[jax.ShapeDtypeStruct(size, BF16) for size in sizes],
        scratch_shapes=[pltpu.VMEM(size, BF16) for size in sizes]
        + [
            pltpu.VMEM((3,) + gate_weight.shape, BF16),
            pltpu.SemaphoreType.DMA((2 * OUTER,)),
            pltpu.SemaphoreType.DMA((6,)),
        ],
        compiler_params=params(60),
        name="pack",
    )(z, gate_weight, up_weight, down_weight.T)

    def shared(block):
        bit = 1
        while 2 * bit < inner:
            other = y_flip(block, bit)
            upper = (y & bit) > 0
            block = jnp.concatenate([jnp.where(upper, other, block), jnp.where(upper, block, other)], 0)
            bit *= 2
        return [block, y_flip(block, bit)]

    y_place = (y >= inner // 2).astype(jnp.int32).reshape(1)

    arrived = {index: z_flip(packed[index], index) for index in (2, 1)}
    blocks = {0: shared(packed[0])}
    w1 = kv_flip(after(out_weight, packed[0]), 1)
    own = kv_index.reshape(1)
    keep, send = attention(queries, key_cache, value_cache, after(own, *packed), cache_lengths)
    arrived[3] = z_flip(after(packed[3], arrived[2]), 3)
    other = kv_flip(send, 1)
    half = jax.ShapeDtypeStruct((keep.shape[0], width // 2 + LANES), BF16)
    keep, send = pl.pallas_call(
        join_kernel,
        in_specs=[SMEM, VMEM, VMEM],
        out_specs=[VMEM, VMEM],
        out_shape=[half, half],
        compiler_params=params(60),
        name="join",
    )(after(chip.reshape(1), arrived[2], arrived[1], blocks[0][1], w1), keep, other)
    other = kv_flip(send, 2)
    blocks[1] = shared(after(arrived[1], keep))
    blocks[2] = shared(after(arrived[2], keep))
    tokens = jax.ShapeDtypeStruct(residual_in.shape, BF16)
    partial, send = pl.pallas_call(
        project_kernel,
        in_specs=[SMEM] + [VMEM] * 4,
        out_specs=[VMEM, VMEM],
        out_shape=[jax.ShapeDtypeStruct(residual_in.shape, F32), tokens],
        scratch_shapes=[
            pltpu.VMEM((keep.shape[0], width // 2), BF16),
            pltpu.VMEM((keep.shape[0], width), F32),
        ],
        compiler_params=params(16),
        name="project",
    )(own, keep, other, out_weight, w1)
    other = kv_flip(send, 2)
    normed, residual = pl.pallas_call(
        norm_kernel,
        in_specs=[VMEM] * 4,
        out_specs=[VMEM, VMEM],
        out_shape=[tokens, tokens],
        compiler_params=params(60),
        name="norm",
    )(partial, other, residual_in, norm_gain.reshape(1, width))

    order = (0, 1, 2, 3)
    deep = width // OUTER

    def laid(indices, base, *others):
        spots, parts = [], []
        for index in indices:
            for mine in (True, False):
                spots.append((index * deep - base, deep // 2, mine))
                parts.append(blocks[index][0 if mine else 1])
        return place(parts, spots, after(y_place, *others))

    near = [laid((0, 1), 0, normed)]
    count = residual_in.shape[0]
    ready = after(normed, arrived[3])
    here = {0: normed, 1: z_flip(ready, 1), 3: z_flip(ready, 3)}
    here[2] = z_flip(ready, 2)
    there = {s: kv_flip(here[s], 2) for s in order}
    blocks[3] = shared(after(arrived[3], blocks[2][1], normed))
    near.append(laid((2, 3), 2 * deep, there[0], there[1], here[3]))
    weights = near + [kv_flip(part, 1) for part in near]

    def added(a, b):
        return (a.astype(F32) + b.astype(F32)).astype(BF16)

    mlp = residual.astype(F32)
    kept, arrivals, terms = [], [], []
    for s in (3, 1, 2, 0):
        turn = after(z, *kept[-1:], *arrivals[:-1], *terms[:-2])
        keep, send = feed(main, tail, order, turn, [here[s], there[s]], weights)
        other = kv_flip(send, 2)
        kept.append(keep)
        arrivals.append(other)
        term = added(keep, other)
        terms.append(z_flip(term, s) if s else term)
        mlp = mlp + terms[-1].astype(F32)
    return mlp.astype(BF16)


def solution(mesh):
    placed = (
        P(("dp", "kv"), None),
        P("dp", None),
        P("dp", "kv", None),
        P("dp", "kv", None),
        P("dp"),
        P("kv", None),
        P(),
        P("dp", "kv"),
        P("dp", "kv"),
        P("kv", "dp"),
    )
    return jax.shard_map(
        per_device, mesh=mesh, in_specs=placed, out_specs=P(("dp", "kv"), None), check_vma=False
    )
```
